256 devices in a mesh: ctx: 64 (over z, y, core), head: 4 (over x).
Axes of the slice: x: 4, y: 4, z: 8, core: 2. Of those that a mesh axis runs over, the one named last changes fastest.
Arguments:
- queries: bfloat16 [32768, 32, 128], P(('ctx', 'head')), may hold values from -100 to 100
- keys: bfloat16 [32768, 4, 128], P(('ctx', 'head')), may hold values from -5 to 5
- values: bfloat16 [32768, 4, 128], P(('ctx', 'head')), may hold values from -6 to 6
- out_grad: bfloat16 [32768, 32, 128], P(('ctx', 'head')), may hold values from -6 to 6
- doc_ids: int32 [32768], replicated, may hold values from 0 to 63, never falling along the last dimension, each value on 1 to 1536 neighbouring positions
Outputs:
- attended: bfloat16 [32768, 32, 128], P(('ctx', 'head'))
- query_grad: bfloat16 [32768, 32, 128], P(('ctx', 'head'))
- key_grad: bfloat16 [32768, 4, 128], P(('ctx', 'head'))
- value_grad: bfloat16 [32768, 4, 128], P(('ctx', 'head'))
The draws below stay inside these ranges and needn't reach their ends.
Inputs may be any that keep to these rules, and one draw needn't show every extreme that they name: `doc_ids`: document numbers never fall along the tokens; each document holds 1 to 1536 tokens, one exactly that many.
All inputs are finite; a program needn't handle non-finite values.
Results may differ from the reference program's by a relative error of at most 0.035.
Values may be sent and summed in bfloat16 or wider, within the bound.
No kernel may reach another device: no remote copies, remote signals or barrier semaphores. Data moves between devices by JAX's collectives and lax.ppermute only.
A program may use at most 64 MiB of HBM per device.

```python
import math
import jax
import jax.numpy as jnp
import numpy as np
from jax import lax

HQ = 32
KVH = 4
HD = 128
NBACK = 3
SHARD = 512
TOKENS = 32768
DOCS = 64
N_CTX = 64


def shared_keys(key):
    return jnp.clip(jax.random.normal(key, (TOKENS, KVH, HD), jnp.float32), -5.0, 5.0)


def draw_keys(key, part):
    base = shared_keys(key)
    return base.astype(jnp.bfloat16)


def draw_queries(key, part):
    key = jax.random.fold_in(key, 7)
    fresh = jnp.clip(jax.random.normal(key, (TOKENS, HQ, HD), jnp.float32), -5.0, 5.0)
    return fresh.astype(jnp.bfloat16)


def shard_levels(stream_key, extent, split, least, high):
    def one(dim, parts):
        draws = jax.random.uniform(jax.random.fold_in(jax.random.fold_in(stream_key, 6), dim), (parts,), jnp.float32, least / len(split), high / len(split))
        return jnp.repeat(jnp.exp(draws), extent[dim] // parts).reshape((-1,) + (1,) * (len(extent) - dim - 1))

    gain = one(*split[0])
    for cut in split[1:]:
        gain = gain * one(*cut)
    return gain


def split_up(number_of, total, most, slope):
    portions = [(1 << 20) // math.isqrt(rank ** slope) + 1 for rank in range(2, number_of + 1)]
    surplus, given = total - most - (number_of - 1), [1] * (number_of - 1)
    while surplus > 0:
        movable = [i for i in range(number_of - 1) if given[i] < most]
        mass, left = sum([portions[i] for i in movable]), surplus
        for i in movable:
            addition = min(most - given[i], max(1, left * portions[i] // mass), surplus)
            given[i] = given[i] + addition
            surplus = surplus - addition
    return np.array([most] + given)


def uneven(own_key, number_of, total, limit, slope):
    if number_of == 2:
        one = jax.random.randint(own_key, (), max(1, total - limit), min(limit, total - 1) + 1)
        return jnp.stack([one, total - one])
    tallies = jnp.asarray(split_up(number_of, total, limit, slope), jnp.int32)
    couples = (number_of - 1) // 2
    source_of, taker = tallies[1:1 + 2 * couples:2], tallies[2:2 + 2 * couples:2]
    room = jnp.minimum(source_of - 1, limit - taker)
    passed = jax.random.randint(jax.random.fold_in(own_key, 1), (couples,), 0, 1 << 20) % (room + 1)
    tallies = tallies.at[1:1 + 2 * couples:2].set(source_of - passed).at[2:2 + 2 * couples:2].set(taker + passed)
    return tallies[jax.random.permutation(jax.random.fold_in(own_key, 2), number_of)]


def gaussian(key, extent, deviation, bound, pieces=(), kind=jnp.bfloat16):
    drawn = deviation * jax.random.normal(key, extent, jnp.float32)
    if pieces:
        drawn = drawn * shard_levels(key, extent, pieces, -0.22, 0.18)
    return jnp.clip(drawn, -bound, bound).astype(kind)


def setup_inputs(seed: int = 0) -> dict:
    arg_keys = jax.random.split(jax.random.key(seed), 6)
    queries = draw_queries(jax.random.fold_in(arg_keys[5], 71), 0)
    keys = draw_keys(jax.random.fold_in(arg_keys[5], 71), 0)
    values = gaussian(arg_keys[2], (TOKENS, KVH, HD), 1.0, 6.0, ((0, 256),))
    out_grad = gaussian(arg_keys[3], (TOKENS, HQ, HD), 1.0, 6.0, ((0, 256),))
    doc_ids = jnp.searchsorted(jnp.cumsum(uneven(arg_keys[4], DOCS, TOKENS, NBACK * SHARD, 1)), jnp.arange(TOKENS), side="right").astype(jnp.int32)
    return {"queries": queries, "keys": keys, "values": values, "out_grad": out_grad, "doc_ids": doc_ids}


def reference(queries, keys, values, out_grad, doc_ids):
    group_size = HQ // KVH
    factor = HD ** -0.5
    front = NBACK * SHARD
    window = front + SHARD
    pad_rows = jnp.zeros((front, KVH, HD), jnp.bfloat16)
    keys_pad = jnp.concatenate([pad_rows, keys], 0)
    values_pad = jnp.concatenate([pad_rows, values], 0)
    tags_pad = jnp.concatenate([jnp.full((front,), -1, jnp.int32), doc_ids.astype(jnp.int32)], 0)
    row_index = jnp.arange(SHARD)[:, None]
    col_index = jnp.arange(window)[None, :] - front
    causal = col_index <= row_index

    def one_shard(totals, index):
        start = (index * SHARD).astype(jnp.int32)
        query = lax.dynamic_slice_in_dim(queries, start, SHARD, 0).astype(jnp.float32).reshape(SHARD, KVH, group_size, HD)
        grad_rows = lax.dynamic_slice_in_dim(out_grad, start, SHARD, 0).astype(jnp.float32).reshape(SHARD, KVH, group_size, HD)
        key_win = lax.dynamic_slice_in_dim(keys_pad, start, window, 0).astype(jnp.float32)
        value_win = lax.dynamic_slice_in_dim(values_pad, start, window, 0).astype(jnp.float32)
        tag_win = lax.dynamic_slice_in_dim(tags_pad, start, window, 0)
        allowed = (tag_win[front:][:, None] == tag_win[None, :]) & causal
        scores = jnp.einsum('skgd,wkd->kgsw', query, key_win) * factor
        scores = jnp.where(allowed, scores, -jnp.inf)
        largest = jnp.max(scores, axis=-1, keepdims=True)
        expo = jnp.exp(scores - largest)
        probs = expo / jnp.sum(expo, axis=-1, keepdims=True)
        probs_low = lax.optimization_barrier(probs.astype(jnp.bfloat16)).astype(jnp.float32)
        attended = jnp.einsum('kgsw,wkd->skgd', probs_low, value_win).astype(jnp.bfloat16)
        dprobs = jnp.einsum('skgd,wkd->kgsw', grad_rows, value_win)
        delta = jnp.einsum('skgd,skgd->kgs', grad_rows, attended.astype(jnp.float32))
        dscores = lax.optimization_barrier((probs * (dprobs - delta[..., None])).astype(jnp.bfloat16)).astype(jnp.float32)
        query_grad = (jnp.einsum('kgsw,wkd->skgd', dscores, key_win) * factor).astype(jnp.bfloat16)
        key_part = jnp.einsum('kgsw,skgd->wkd', dscores, query) * factor
        value_part = jnp.einsum('kgsw,skgd->wkd', probs_low, grad_rows)
        key_tot = lax.dynamic_update_slice_in_dim(totals[0], lax.dynamic_slice_in_dim(totals[0], start, window, 0) + key_part, start, 0)
        value_tot = lax.dynamic_update_slice_in_dim(totals[1], lax.dynamic_slice_in_dim(totals[1], start, window, 0) + value_part, start, 0)
        return (key_tot, value_tot), (attended.reshape(SHARD, HQ, HD), query_grad.reshape(SHARD, HQ, HD))

    zero_sums = jnp.zeros((front + TOKENS, KVH, HD), jnp.float32)
    (key_all, value_all), (outputs, query_all) = lax.scan(one_shard, (zero_sums, zero_sums), jnp.arange(N_CTX, dtype=jnp.int32))
    return (outputs.reshape(TOKENS, HQ, HD), query_all.reshape(TOKENS, HQ, HD),
            key_all[front:].astype(jnp.bfloat16), value_all[front:].astype(jnp.bfloat16))
```

```python
import functools
import math

import jax
import jax.numpy as jnp
from jax import lax
from jax.experimental import pallas as pl
from jax.experimental.pallas import tpu as pltpu
from jax.sharding import PartitionSpec as P

HQ = 32
KVH = 4
HD = 128
NBACK = 3
GROUP = HQ // KVH
FACTOR = HD ** -0.5
EXP_SCALE = FACTOR * math.log2(math.e)
NEG = -1e30
KT = 256
BF = jnp.bfloat16
F32 = jnp.float32
ANY = pl.BlockSpec(memory_space=pl.ANY)
VM = pl.BlockSpec(memory_space=pltpu.VMEM)
SM = pl.BlockSpec(memory_space=pltpu.SMEM)


def params(mb=56):
    return pltpu.CompilerParams(vmem_limit_bytes=mb << 20)


def dot(a, b):
    return lax.dot_general(a, b, (((1,), (0,)), ((), ())), preferred_element_type=F32)


def pack_kernel(n, info, src, *rest):
    outs, scr = rest[:n], rest[n]
    scr[...] = src[...].astype(F32)
    for e in range(n):
        h = lax.rem(info[0] + e, n)
        blk = scr[:, pl.ds(pl.multiple_of(h * GROUP, GROUP), GROUP), :]
        outs[e][...] = blk.reshape(-1, HD).astype(BF)


def pack(info, arr, n):
    tok = arr.shape[0]
    step = 32
    return pl.pallas_call(
        functools.partial(pack_kernel, n),
        grid_spec=pltpu.PrefetchScalarGridSpec(
            num_scalar_prefetch=1,
            grid=(tok // step,),
            in_specs=[pl.BlockSpec((step, HQ, HD), lambda i, s: (i, 0, 0))],
            out_specs=[pl.BlockSpec((step * GROUP, HD), lambda i, s: (i, 0))] * n,
            scratch_shapes=[pltpu.VMEM((step, HQ, HD), F32)],
        ),
        out_shape=[jax.ShapeDtypeStruct((tok * GROUP, HD), BF)] * n,
        name="pack",
    )(info, arr)


def unpack_kernel(n, info, *rest):
    srcs, out, scr = rest[:n], rest[n], rest[n + 1]
    for e in range(n):
        h = lax.rem(info[0] + e, n)
        blk = srcs[e][...].astype(F32).reshape(-1, GROUP, HD)
        scr[:, pl.ds(pl.multiple_of(h * GROUP, GROUP), GROUP), :] = blk
    out[...] = scr[...].astype(BF)


def unpack(info, parts):
    n = len(parts)
    tok = parts[0].shape[0] // GROUP
    step = 32
    return pl.pallas_call(
        functools.partial(unpack_kernel, n),
        grid_spec=pltpu.PrefetchScalarGridSpec(
            num_scalar_prefetch=1,
            grid=(tok // step,),
            in_specs=[pl.BlockSpec((step * GROUP, HD), lambda i, s: (i, 0))] * n,
            out_specs=pl.BlockSpec((step, HQ, HD), lambda i, s: (i, 0, 0)),
            scratch_shapes=[pltpu.VMEM((step, HQ, HD), F32)],
        ),
        out_shape=jax.ShapeDtypeStruct((tok, HQ, HD), BF),
        name="unpack",
    )(info, *parts)


def masked_scores(k, qt, start, pos, base):
    s = dot(k, qt)
    u = base + lax.broadcasted_iota(jnp.int32, s.shape, 0)
    return jnp.where((u >= start) & (u <= pos), s, NEG)


def positions(block, first, rows):
    lane = lax.broadcasted_iota(jnp.int32, (1, rows), 1)
    return first + block * (rows // GROUP) + lane // GROUP


def fwd_kernel(n, shard, info, start_ref, *refs):
    q_in = refs[:n]
    kv_in = refs[n : n + NBACK + 1]
    att, qt_out, ot_out, stat_out = refs[n + NBACK + 1 : n + NBACK + 5]
    k_scr, vt_scr, s_scr, acc, q_scr, sems = refs[n + NBACK + 5 :]
    rows = q_scr.shape[1]
    tiles_per = shard // KT
    front = NBACK * shard
    copies = [pltpu.make_async_copy(q_in[e], q_scr.at[e], sems.at[e]) for e in range(n)]
    for c in copies:
        c.start()
    for d in range(NBACK + 1):
        for t in range(tiles_per):
            at = (NBACK - d) * tiles_per + t
            k_scr[at] = kv_in[d][0, t * KT : (t + 1) * KT, :]
            vt_scr[at] = kv_in[d][1, t * KT : (t + 1) * KT, :].T
    for c in copies:
        c.wait()

    def block(e, carry):
        i = lax.rem(info[0] - e + n, n)
        lo = info[1 + i]
        hi = (front + (i + 1) * (rows // GROUP) + KT - 1) // KT
        start = start_ref[i]
        pos = positions(i, front, rows)
        qt = q_scr[e].T
        qt_out[e] = qt

        def scores(j, m):
            s = masked_scores(k_scr[j], qt, start, pos, j * KT)
            s_scr[j] = s
            return jnp.maximum(m, jnp.max(s.reshape(KT // 8, 8, rows), axis=0))

        m8 = lax.fori_loop(lo, hi, scores, jnp.full((8, rows), NEG, F32))
        m = jnp.max(m8, axis=0, keepdims=True)
        acc[...] = jnp.zeros_like(acc)

        def weigh(j, l):
            p = jnp.exp2((s_scr[j] - m) * EXP_SCALE)
            acc[...] += dot(vt_scr[j], p.astype(BF))
            return l + jnp.sum(p.reshape(KT // 8, 8, rows), axis=0)

        l8 = lax.fori_loop(lo, hi, weigh, jnp.zeros((8, rows), F32))
        rl = 1.0 / jnp.sum(l8, axis=0, keepdims=True)
        ot = (acc[...] * rl).astype(BF)
        ot_out[e] = ot
        att[e] = ot.T
        stat_out[e] = jnp.concatenate([m, rl], axis=0)
        return carry

    lax.fori_loop(0, n, block, 0)


def forward(info, start, q_slots, kvs):
    n = len(q_slots)
    rows = q_slots[0].shape[0]
    shard = kvs[0].shape[1]
    tiles = (NBACK + 1) * shard // KT
    outs = [
        jax.ShapeDtypeStruct((n, rows, HD), BF),
        jax.ShapeDtypeStruct((n, HD, rows), BF),
        jax.ShapeDtypeStruct((n, HD, rows), BF),
        jax.ShapeDtypeStruct((n, 2, rows), F32),
    ]
    return pl.pallas_call(
        functools.partial(fwd_kernel, n, shard),
        in_specs=[SM, VM] + [ANY] * n + [VM] * (NBACK + 1),
        out_specs=[VM] * 4,
        out_shape=outs,
        scratch_shapes=[
            pltpu.VMEM((tiles, KT, HD), BF),
            pltpu.VMEM((tiles, HD, KT), BF),
            pltpu.VMEM((tiles, KT, rows), F32),
            pltpu.VMEM((HD, rows), F32),
            pltpu.VMEM((n, rows, HD), BF),
            pltpu.SemaphoreType.DMA((n,)),
        ],
        compiler_params=params(),
        cost_estimate=pl.CostEstimate(flops=8 << 30, bytes_accessed=8 << 20, transcendentals=8 << 20),
        name="forward",
    )(info, start, *q_slots, *kvs)


def bwd_kernel(n, shard, first_tile, n_kv, has_part, last, info, start_ref, *refs):
    q_in, g_in = refs[:n], refs[n : 2 * n]
    qt_ref, ot_ref, stat_ref = refs[2 * n : 2 * n + 3]
    p = 2 * n + 3
    kv_in = refs[p : p + n_kv]
    p += n_kv
    if has_part:
        part_in = refs[p]
        p += 1
    dq_out, dkv_out = refs[p], refs[p + 1]
    k_scr, v_scr, kt_scr, dk, dv, acc, q_scr, g_scr, sems = refs[p + 2 :]
    rows = q_scr.shape[1]
    tiles_per = shard // KT
    tiles = n_kv * tiles_per
    front = NBACK * shard
    copies = []
    for e in range(n):
        copies.append(pltpu.make_async_copy(q_in[e], q_scr.at[e], sems.at[e]))
        copies.append(pltpu.make_async_copy(g_in[e], g_scr.at[e], sems.at[n + e]))
    for c in copies:
        c.start()
    for d in range(n_kv):
        for t in range(tiles_per):
            at = (n_kv - 1 - d) * tiles_per + t
            k = kv_in[d][0, t * KT : (t + 1) * KT, :]
            k_scr[at] = k
            kt_scr[at] = k.T
            v_scr[at] = kv_in[d][1, t * KT : (t + 1) * KT, :]
    dk[...] = jnp.zeros_like(dk)
    dv[...] = jnp.zeros_like(dv)
    for c in copies:
        c.wait()

    def block(e, carry):
        i = lax.rem(info[0] - e + n, n)
        lo = jnp.maximum(info[1 + i] - first_tile, 0)
        hi = jnp.minimum((front + (i + 1) * (rows // GROUP) + KT - 1) // KT - first_tile, tiles)
        start = start_ref[i]
        pos = positions(i, front, rows)
        if has_part:
            acc[...] = part_in[e]
        else:
            acc[...] = jnp.zeros_like(acc)

        @pl.when(lo < hi)
        def _():
            qt = qt_ref[e]
            q = q_scr[e]
            g = g_scr[e]
            gt = g.T
            delta = jnp.sum(gt.astype(F32) * ot_ref[e].astype(F32), axis=0, keepdims=True)
            stat = stat_ref[e]
            m, rl = stat[0:1], stat[1:2]

            def tile(j, c):
                s = masked_scores(k_scr[j], qt, start, pos, (j + first_tile) * KT)
                probs = jnp.exp2((s - m) * EXP_SCALE) * rl
                dprobs = dot(v_scr[j], gt)
                ds = (probs * (dprobs - delta)).astype(BF)
                dv[j] += dot(probs.astype(BF), g)
                dk[j] += dot(ds, q)
                acc[...] += dot(kt_scr[j], ds)
                return c

            lax.fori_loop(lo, hi, tile, 0)

        if last:
            dq_out[e] = (acc[...] * FACTOR).astype(BF).T
        else:
            dq_out[e] = acc[...]
        return carry

    lax.fori_loop(0, n, block, 0)
    for d in range(n_kv):
        for t in range(tiles_per):
            at = (n_kv - 1 - d) * tiles_per + t
            dkv_out[d, 0, t * KT : (t + 1) * KT, :] = (dk[at] * FACTOR).astype(dkv_out.dtype)
            dkv_out[d, 1, t * KT : (t + 1) * KT, :] = dv[at].astype(dkv_out.dtype)


def backward(info, start, q_slots, g_slots, saved, kvs, first_tile, part, last, kind):
    n = len(q_slots)
    rows = q_slots[0].shape[0]
    shard = kvs[0].shape[1]
    n_kv = len(kvs)
    tiles = n_kv * shard // KT
    has_part = part is not None
    dq = jax.ShapeDtypeStruct((n, rows, HD), BF) if last else jax.ShapeDtypeStruct((n, HD, rows), F32)
    return pl.pallas_call(
        functools.partial(bwd_kernel, n, shard, first_tile, n_kv, has_part, last),
        in_specs=[SM, VM] + [ANY] * (2 * n) + [VM] * (3 + n_kv + has_part),
        out_specs=[VM] * 2,
        out_shape=[dq, jax.ShapeDtypeStruct((n_kv, 2, shard, HD), kind)],
        scratch_shapes=[
            pltpu.VMEM((tiles, KT, HD), BF),
            pltpu.VMEM((tiles, KT, HD), BF),
            pltpu.VMEM((tiles, HD, KT), BF),
            pltpu.VMEM((tiles, KT, HD), F32),
            pltpu.VMEM((tiles, KT, HD), F32),
            pltpu.VMEM((HD, rows), F32),
            pltpu.VMEM((n, rows, HD), BF),
            pltpu.VMEM((n, rows, HD), BF),
            pltpu.SemaphoreType.DMA((2 * n,)),
        ],
        compiler_params=params(),
        cost_estimate=pl.CostEstimate(flops=10 << 30, bytes_accessed=8 << 20, transcendentals=8 << 20),
        name="backward_own" if last else "backward_halo",
    )(info, start, *q_slots, *g_slots, *saved, *kvs, *([part] if has_part else []))


def around(value, shift, n):
    if shift % n == 0:
        return value
    return lax.ppermute(value, "head", [(i, (i + shift) % n) for i in range(n)])


def along(value, steps, starts):
    count = lax.axis_size("ctx")
    pairs = [(c, c + steps) for c in starts if 0 <= c + steps < count]
    return lax.ppermute(value, "ctx", pairs)


def shards(queries, keys, values, out_grad, doc_ids):
    n = lax.axis_size("head")
    n_ctx = lax.axis_size("ctx")
    tok = queries.shape[0]
    shard = tok * n
    front = NBACK * shard
    x = lax.axis_index("head")
    ctx = lax.axis_index("ctx")
    core = lax.rem(ctx, 2)
    everyone, even, odd = range(n_ctx), range(0, n_ctx, 2), range(1, n_ctx, 2)

    kv = jnp.stack([keys, values]).transpose(2, 0, 1, 3)
    kv_parts = [
        around(lax.dynamic_index_in_dim(kv, lax.rem(x + e, n), 0, keepdims=False), e, n) for e in range(n)
    ]
    ring = jnp.concatenate(kv_parts[::-1] + kv_parts[::-1], axis=1)
    own = lax.dynamic_slice_in_dim(ring, (n - 1 - x) * tok, shard, 1)

    tags_pad = jnp.concatenate([jnp.full((front,), -1, jnp.int32), doc_ids], 0)
    window = lax.dynamic_slice_in_dim(tags_pad, ctx * shard, front + shard, 0)
    start = jnp.sum((window[None, :] < window[front:, None]).astype(jnp.int32), axis=1)
    info = jnp.concatenate([x[None].astype(jnp.int32), start[::tok] // KT])
    start_rows = jnp.repeat(start.reshape(n, 1, tok), GROUP, axis=2)

    xi = x[None].astype(jnp.int32)
    q_slots = [around(v, e, n) for e, v in enumerate(pack(xi, queries, n))]
    g_slots = [around(v, e, n) for e, v in enumerate(pack(xi, out_grad, n))]

    behind = along(own, 2, everyone)
    far = along(own, 3, odd)
    swap = [(c, c ^ 1) for c in everyone]
    own_swap = lax.ppermute(own, "ctx", swap)
    behind_swap = lax.ppermute(behind, "ctx", swap)
    first = core == 0
    kvs = [own, jnp.where(first, behind_swap, own_swap), behind, jnp.where(first, far, behind_swap)]

    att, qt, ot, stat = forward(info, start_rows, q_slots, kvs)
    att_parts = [around(att[e], -e, n) for e in range(n)]

    saved = (qt, ot, stat)
    part, halo = backward(info, start_rows, q_slots, g_slots, saved, kvs[1:], 0, None, False, BF)
    d1, d2, d3 = halo[0], halo[1], halo[2]
    cross = lax.ppermute(jnp.where(first, d1, d3), "ctx", swap)
    beside = lax.ppermute(d1, "ctx", [(c, c - 1) for c in odd])
    back = along((d2.astype(F32) + cross.astype(F32)).astype(BF), -2, everyone)
    back_far = along(d3, -3, even)

    dq, mine = backward(
        info, start_rows, q_slots, g_slots, saved, kvs[:1], NBACK * shard // KT, part, True, F32
    )
    dq_parts = [around(dq[e], -e, n) for e in range(n)]
    total = mine[0] + back.astype(F32) + beside.astype(F32) + back_far.astype(F32)
    total = total.astype(BF).reshape(2, n, tok, HD)
    pieces = [
        around(lax.dynamic_index_in_dim(total, lax.rem(x + e, n), 1, keepdims=False), e, n) for e in range(n)
    ]
    ring = jnp.stack(pieces[::-1] + pieces[::-1], axis=0)
    heads = lax.dynamic_slice_in_dim(ring, n - 1 - x, n, 0).transpose(1, 2, 0, 3)

    return unpack(xi, att_parts), unpack(xi, dq_parts), heads[0], heads[1]


def solution(mesh):
    spec = P(("ctx", "head"), None, None)
    return jax.shard_map(
        shards,
        mesh=mesh,
        in_specs=(spec, spec, spec, spec, P()),
        out_specs=(spec, spec, spec, spec),
        check_vma=False,
    )
```

```python
import functools
import math

import jax
import jax.numpy as jnp
from jax import lax
from jax.experimental import pallas as pl
from jax.experimental.pallas import tpu as pltpu
from jax.sharding import PartitionSpec as P

HQ = 32
KVH = 4
HD = 128
NBACK = 3
GROUP = HQ // KVH
FACTOR = HD ** -0.5
EXP_SCALE = FACTOR * math.log2(math.e)
NEG = -1e30
FT = 512
HT = 512
OT = 256
PAD = 512
BF = jnp.bfloat16
F32 = jnp.float32
ANY = pl.BlockSpec(memory_space=pl.ANY)
VM = pl.BlockSpec(memory_space=pltpu.VMEM)
SM = pl.BlockSpec(memory_space=pltpu.SMEM)
LIGHT = pl.CostEstimate(flops=1 << 20, bytes_accessed=1 << 21, transcendentals=0)
HEAVY = pl.CostEstimate(flops=1 << 33, bytes_accessed=8 << 20, transcendentals=1 << 22)


def params(mb=56):
    return pltpu.CompilerParams(vmem_limit_bytes=mb << 20)


def dot(a, b):
    return lax.dot_general(a, b, (((1,), (0,)), ((), ())), preferred_element_type=F32)

def pack_kernel(n, info, src, *rest):
    outs, sems = rest[:n], rest[n]
    copies = [
        pltpu.make_async_copy(src.at[:, lax.rem(info[0] + e, n)], outs[e], sems.at[e]) for e in range(n)
    ]
    for c in copies:
        c.start()
    for c in copies:
        c.wait()


def pack(info, arr, n):
    tok = arr.shape[0]
    return pl.pallas_call(
        functools.partial(pack_kernel, n),
        in_specs=[SM, VM],
        out_specs=[ANY] * n,
        out_shape=[jax.ShapeDtypeStruct((tok, GROUP, HD), BF)] * n,
        scratch_shapes=[pltpu.SemaphoreType.DMA((n,))],
        cost_estimate=LIGHT,
        name="pack",
    )(info, arr.reshape(tok, n, GROUP, HD))


def unpack_kernel(n, info, *rest):
    srcs, out, sems = rest[:n], rest[n], rest[n + 1]
    copies = [
        pltpu.make_async_copy(srcs[e], out.at[:, lax.rem(info[0] + e, n)], sems.at[e]) for e in range(n)
    ]
    for c in copies:
        c.start()
    for c in copies:
        c.wait()


def unpack(info, parts):
    n = len(parts)
    tok = parts[0].shape[0]
    return pl.pallas_call(
        functools.partial(unpack_kernel, n),
        in_specs=[SM] + [ANY] * n,
        out_specs=VM,
        out_shape=jax.ShapeDtypeStruct((tok, n, GROUP, HD), BF),
        scratch_shapes=[pltpu.SemaphoreType.DMA((n,))],
        cost_estimate=LIGHT,
        name="unpack",
    )(info, *parts).reshape(tok, n * GROUP, HD)


def masked_scores(k, qt, start, pos, base):
    s = dot(k, qt)
    u = base + lax.broadcasted_iota(jnp.int32, s.shape, 0)
    return jnp.where((u >= start) & (u <= pos), s, NEG)


def positions(block, first, rows):
    lane = lax.broadcasted_iota(jnp.int32, (1, rows), 1)
    return first + block * (rows // GROUP) + lane // GROUP


def fwd_kernel(n, shard, info, start_ref, *refs):
    q_in = refs[:n]
    kv_in = refs[n : n + NBACK + 1]
    p = n + NBACK + 1
    atts = refs[p : p + n]
    stat_out = refs[p + n]
    k_scr, v_scr, vt_scr, acc, q_scr, o_scr, q_sems, o_sems, kv_sems = refs[p + n + 1 :]
    rows = q_scr.shape[1]
    front = NBACK * shard
    k_in, v_in = [], []
    for d in range(NBACK + 1):
        at = pl.ds(PAD + (NBACK - d) * shard, shard)
        v_in.append(pltpu.make_async_copy(kv_in[d].at[1], v_scr.at[at], kv_sems.at[2 * d + 1]))
        k_in.append(pltpu.make_async_copy(kv_in[d].at[0], k_scr.at[at], kv_sems.at[2 * d]))
        v_in[d].start()
        k_in[d].start()

    def fetch(e):
        pltpu.make_async_copy(q_in[e], q_scr.at[e], q_sems.at[e]).start()

    fetch(0)
    k_scr[:PAD] = jnp.zeros((PAD, HD), BF)
    vt_scr[:, :PAD] = jnp.zeros((HD, PAD), BF)
    for d in range(NBACK + 1):
        at = PAD + (NBACK - d) * shard
        v_in[d].wait()
        vt_scr[:, at : at + shard] = v_scr[at : at + shard].T
    for d in range(NBACK + 1):
        k_in[d].wait()
    half = rows // 2

    def block(e, carry):
        i = lax.rem(info[0] - e + n, n)
        end = front + (i + 1) * (rows // GROUP)
        steps = (end - info[1 + i] + FT - 1) // FT
        start = start_ref[i]
        pos = positions(i, front, rows)
        pltpu.make_async_copy(q_in[0], q_scr.at[e], q_sems.at[e]).wait()
        for f in range(1, n):
            pl.when(e + 1 == f)(functools.partial(fetch, f))
        qt = q_scr[e].T
        acc[...] = jnp.zeros_like(acc)

        def tile(t, state):
            base = end - (t + 1) * FT
            at = pl.multiple_of(base + PAD, 128)
            k = k_scr[pl.ds(at, FT)]
            vt = vt_scr[:, pl.ds(at, FT)]
            ss = [
                masked_scores(k, qt[:, a : a + half], start[:, a : a + half], pos[:, a : a + half], base)
                for a in (0, half)
            ]
            new = []
            for b, s in enumerate(ss):
                m, l = state[b]
                cols = slice(b * half, (b + 1) * half)
                top = jnp.max(jnp.max(s.reshape(FT // 8, 8, half), axis=0), axis=0, keepdims=True)
                m_new = jnp.maximum(m, top)
                fade = jnp.exp2((m - m_new) * EXP_SCALE)
                w = jnp.exp2((s - m_new) * EXP_SCALE)
                acc[:, cols] = acc[:, cols] * fade + dot(vt, w.astype(BF))
                l = l * fade + jnp.sum(w.reshape(FT // 8, 8, half), axis=0)
                new.append((m_new, l))
            return tuple(new)

        first = (jnp.full((1, half), NEG, F32), jnp.zeros((8, half), F32))
        state = lax.fori_loop(0, steps, tile, (first, first))
        m = jnp.concatenate([state[0][0], state[1][0]], axis=1)
        l = jnp.sum(jnp.concatenate([state[0][1], state[1][1]], axis=1), axis=0, keepdims=True)
        o_scr[e] = (acc[...] * (1.0 / l)).astype(BF).T
        stat_out[e] = m * EXP_SCALE + jnp.log2(l)
        for f in range(n):

            @pl.when(e == f)
            def _():
                pltpu.make_async_copy(o_scr.at[f], atts[f], o_sems.at[f]).start()

        return carry

    lax.fori_loop(0, n, block, 0)
    for e in range(n):
        pltpu.make_async_copy(o_scr.at[e], atts[e], o_sems.at[e]).wait()


def forward(info, start, q_slots, kvs):
    n = len(q_slots)
    rows = q_slots[0].shape[0]
    shard = kvs[0].shape[1]
    keys = (NBACK + 1) * shard + PAD
    return pl.pallas_call(
        functools.partial(fwd_kernel, n, shard),
        in_specs=[SM, VM] + [ANY] * (n + NBACK + 1),
        out_specs=[ANY] * n + [VM],
        out_shape=[jax.ShapeDtypeStruct((rows, HD), BF)] * n + [jax.ShapeDtypeStruct((n, 1, rows), F32)],
        scratch_shapes=[
            pltpu.VMEM((keys, HD), BF),
            pltpu.VMEM((keys, HD), BF),
            pltpu.VMEM((HD, keys), BF),
            pltpu.VMEM((HD, rows), F32),
            pltpu.VMEM((n, rows, HD), BF),
            pltpu.VMEM((n, rows, HD), BF),
            pltpu.SemaphoreType.DMA((n,)),
            pltpu.SemaphoreType.DMA((n,)),
            pltpu.SemaphoreType.DMA((2 * NBACK + 2,)),
        ],
        compiler_params=params(),
        cost_estimate=LIGHT,
        name="forward",
    )(info, start, *q_slots, *kvs)


def bwd_kernel(n, shard, halo, n_kv, step, info, start_ref, stat_ref, *refs):
    q_in, g_in = refs[:n], refs[n : 2 * n]
    p = 2 * n
    kv_in = refs[p : p + n_kv]
    p += n_kv
    if halo:
        o_in = refs[p : p + n]
        p += n
        part_out, delta_ref, cross_out, straight_out, other_out = refs[p : p + 5]
        p += 5
    else:
        part_in, delta_ref = refs[p : p + 2]
        dq_outs = refs[p + 2 : p + 2 + n]
        dkv_out = refs[p + 2 + n]
        p += n + 3
    k_scr, v_scr, kt_scr, dk, dv, acc, q_scr, g_scr, o_scr, p_scr, ds_scr = refs[p : p + 11]
    q_sems, g_sems, o_sems, kv_sems, a_sems = refs[p + 11 :]
    rows = q_scr.shape[1]
    front = NBACK * shard
    first_key = 0 if halo else front
    k_copy, v_copy = [], []
    for d in range(n_kv):
        at = pl.ds(PAD + (n_kv - 1 - d) * shard, shard)
        k_copy.append(pltpu.make_async_copy(kv_in[d].at[0], k_scr.at[at], kv_sems.at[2 * d]))
        v_copy.append(pltpu.make_async_copy(kv_in[d].at[1], v_scr.at[at], kv_sems.at[2 * d + 1]))
        k_copy[d].start()
        v_copy[d].start()

    def fetch(e):
        pltpu.make_async_copy(q_in[e], q_scr.at[e], q_sems.at[e]).start()
        pltpu.make_async_copy(g_in[e], g_scr.at[e], g_sems.at[e]).start()
        if halo:
            pltpu.make_async_copy(o_in[e], o_scr.at[e], o_sems.at[e]).start()
        else:
            pltpu.make_async_copy(part_in.at[e], acc.at[e], a_sems.at[e]).start()

    fetch(0)
    k_scr[:PAD] = jnp.zeros((PAD, HD), BF)
    v_scr[:PAD] = jnp.zeros((PAD, HD), BF)
    kt_scr[:, :PAD] = jnp.zeros((HD, PAD), BF)
    dk[...] = jnp.zeros_like(dk)
    dv[...] = jnp.zeros_like(dv)
    for d in range(n_kv):
        at = PAD + (n_kv - 1 - d) * shard
        k_copy[d].wait()
        kt_scr[:, at : at + shard] = k_scr[at : at + shard].T
    for d in range(n_kv):
        v_copy[d].wait()
    half = rows // 2

    def block(e, carry):
        i = lax.rem(info[0] - e + n, n)
        end = front if halo else front + (i + 1) * (rows // GROUP)
        low = jnp.maximum(info[1 + i], first_key)
        steps = jnp.maximum(end - low + step - 1, 0) // step
        start = jnp.maximum(start_ref[i], first_key)
        pos = positions(i, front, rows)
        pltpu.make_async_copy(q_in[0], q_scr.at[e], q_sems.at[e]).wait()
        pltpu.make_async_copy(g_in[0], g_scr.at[e], g_sems.at[e]).wait()
        if halo:
            pltpu.make_async_copy(o_in[0], o_scr.at[e], o_sems.at[e]).wait()
        else:
            pltpu.make_async_copy(part_in.at[0], acc.at[e], a_sems.at[e]).wait()
        for f in range(1, n):
            pl.when(e + 1 == f)(functools.partial(fetch, f))
        gt = g_scr[e].T
        if halo:
            acc[e] = jnp.zeros((HD, rows), F32)
            delta = jnp.sum(gt.astype(F32) * o_scr[e].T.astype(F32), axis=0, keepdims=True)
            delta_ref[e] = delta
        else:
            delta = delta_ref[e]

        @pl.when(steps > 0)
        def _():
            q = q_scr[e]
            g = g_scr[e]
            qt = q.T
            stat = stat_ref[e]

            def tile(t, c):
                base = end - (t + 1) * step
                at = pl.multiple_of(base - first_key + PAD, 128)
                ds_at = pl.ds(at, step)
                k = k_scr[ds_at]
                v = v_scr[ds_at]
                for a in (0, half):
                    cols = slice(a, a + half)
                    s = masked_scores(k, qt[:, cols], start[:, cols], pos[:, cols], base)
                    dp = dot(v, gt[:, cols])
                    w = jnp.exp2(s * EXP_SCALE - stat[:, cols])
                    p_scr[:, cols] = w.astype(BF)
                    ds_scr[:, cols] = (w * (dp - delta[:, cols])).astype(BF)
                dv[ds_at] += dot(p_scr[...], g)
                dk[ds_at] += dot(ds_scr[...], q)
                acc[e] += dot(kt_scr[:, ds_at], ds_scr[...])
                return c

            lax.fori_loop(0, steps, tile, 0)

        if not halo:
            o_scr[e] = (acc[e] * FACTOR).astype(BF).T
        for f in range(n):

            @pl.when(e == f)
            def _():
                if halo:
                    pltpu.make_async_copy(acc.at[f], part_out.at[f], a_sems.at[f]).start()
                else:
                    pltpu.make_async_copy(o_scr.at[f], dq_outs[f], o_sems.at[f]).start()

        return carry

    lax.fori_loop(0, n, block, 0)

    def give(ref, d):
        at = PAD + (n_kv - 1 - d) * shard
        ref[0] = (dk[at : at + shard] * FACTOR).astype(ref.dtype)
        ref[1] = dv[at : at + shard].astype(ref.dtype)

    if halo:
        give(straight_out, 1)

        @pl.when(info[n + 1] == 0)
        def _():
            give(cross_out, 0)
            give(other_out, 2)

        @pl.when(info[n + 1] == 1)
        def _():
            give(cross_out, 2)
            give(other_out, 0)

        for e in range(n):
            pltpu.make_async_copy(acc.at[e], part_out.at[e], a_sems.at[e]).wait()
    else:
        give(dkv_out, 0)
        for e in range(n):
            pltpu.make_async_copy(o_scr.at[e], dq_outs[e], o_sems.at[e]).wait()


def backward(info, start, q_slots, g_slots, stat, kvs, o_slots=None, part=None, delta=None):
    n = len(q_slots)
    rows = q_slots[0].shape[0]
    shard = kvs[0].shape[1]
    n_kv = len(kvs)
    halo = part is None
    step = HT if halo else OT
    keys = n_kv * shard + PAD
    delta_shape = jax.ShapeDtypeStruct((n, 1, rows), F32)
    if halo:
        extra, extra_specs = list(o_slots), [ANY] * n
        outs = [jax.ShapeDtypeStruct((n, HD, rows), F32), delta_shape]
        outs += [jax.ShapeDtypeStruct((2, shard, HD), BF)] * 3
        out_specs = [ANY] + [VM] * 4
    else:
        extra, extra_specs = [part, delta], [ANY, VM]
        outs = [jax.ShapeDtypeStruct((rows, HD), BF)] * n + [jax.ShapeDtypeStruct((2, shard, HD), F32)]
        out_specs = [ANY] * n + [VM]
    return pl.pallas_call(
        functools.partial(bwd_kernel, n, shard, halo, n_kv, step),
        in_specs=[SM, VM, VM] + [ANY] * (2 * n + n_kv) + extra_specs,
        out_specs=out_specs,
        out_shape=outs,
        scratch_shapes=[
            pltpu.VMEM((keys, HD), BF),
            pltpu.VMEM((keys, HD), BF),
            pltpu.VMEM((HD, keys), BF),
            pltpu.VMEM((keys, HD), F32),
            pltpu.VMEM((keys, HD), F32),
            pltpu.VMEM((n, HD, rows), F32),
            pltpu.VMEM((n, rows, HD), BF),
            pltpu.VMEM((n, rows, HD), BF),
            pltpu.VMEM((n, rows, HD), BF),
            pltpu.VMEM((step, rows), BF),
            pltpu.VMEM((step, rows), BF),
            pltpu.SemaphoreType.DMA((n,)),
            pltpu.SemaphoreType.DMA((n,)),
            pltpu.SemaphoreType.DMA((n,)),
            pltpu.SemaphoreType.DMA((2 * n_kv,)),
            pltpu.SemaphoreType.DMA((n,)),
        ],
        compiler_params=params(),
        cost_estimate=LIGHT,
        name="backward_halo" if halo else "backward_own",
    )(info, start, stat, *q_slots, *g_slots, *kvs, *extra)


def around(value, shift, n):
    if shift % n == 0:
        return value
    return lax.ppermute(value, "head", [(i, (i + shift) % n) for i in range(n)])


def along(value, steps, starts):
    count = lax.axis_size("ctx")
    pairs = [(c, c + steps) for c in starts if 0 <= c + steps < count]
    return lax.ppermute(value, "ctx", pairs)


def shards(queries, keys, values, out_grad, doc_ids):
    n = lax.axis_size("head")
    n_ctx = lax.axis_size("ctx")
    tok = queries.shape[0]
    shard = tok * n
    front = NBACK * shard
    x = lax.axis_index("head")
    ctx = lax.axis_index("ctx")
    core = lax.rem(ctx, 2)
    everyone, even, odd = range(n_ctx), range(0, n_ctx, 2), range(1, n_ctx, 2)
    swap = [(c, c ^ 1) for c in everyone]
    first = core == 0
    xi = x[None].astype(jnp.int32)
    order = (2, 1, 3)

    kv = jnp.stack([keys, values]).transpose(2, 0, 1, 3)
    kv_parts = {0: lax.dynamic_index_in_dim(kv, x, 0, keepdims=False)}
    for e in order:
        kv_parts[e] = around(lax.dynamic_index_in_dim(kv, lax.rem(x + e, n), 0, keepdims=False), e, n)

    def slots(packed):
        got = {e: around(packed[e], e, n) for e in order}
        return [packed[0]] + [got[e] for e in range(1, n)]

    def packed(arr):
        return [v.reshape(tok * GROUP, HD) for v in pack(xi, arr, n)]

    q_packed, g_packed = packed(queries), packed(out_grad)
    kv_parts = lax.optimization_barrier((kv_parts, q_packed, g_packed))[0]
    q_slots = slots(q_packed)
    g_slots = slots(g_packed)

    ring = [kv_parts[e] for e in range(n - 1, -1, -1)]
    own = lax.dynamic_slice_in_dim(jnp.concatenate(ring + ring, axis=1), (n - 1 - x) * tok, shard, 1)

    tags_pad = jnp.concatenate([jnp.full((front,), -1, jnp.int32), doc_ids], 0)
    window = lax.dynamic_slice_in_dim(tags_pad, ctx * shard, front + shard, 0)
    start = jnp.sum((window[None, :] < window[front:, None]).astype(jnp.int32), axis=1)
    info = jnp.concatenate([xi, start[::tok], core[None].astype(jnp.int32)])
    start_rows = jnp.repeat(start.reshape(n, 1, tok), GROUP, axis=2)

    behind = along(own, 2, everyone)
    far = along(own, 3, odd)
    own_swap = lax.ppermute(own, "ctx", swap)
    behind_swap = lax.ppermute(behind, "ctx", swap)
    kvs = [own, jnp.where(first, behind_swap, own_swap), behind, jnp.where(first, far, behind_swap)]

    *atts, stat = forward(info, start_rows, q_slots, kvs)
    att_parts = [around(atts[e], -e, n) for e in range(n)]

    part, delta, cross, straight, other = backward(info, start_rows, q_slots, g_slots, stat, kvs[1:], o_slots=atts)
    crossed = lax.ppermute(cross, "ctx", swap)
    summed = (straight.astype(F32) + crossed.astype(F32)).astype(BF)
    info, summed = lax.optimization_barrier((info, summed))
    back = along(summed, -2, everyone)
    back_far = along(other, -3, even)
    beside = lax.ppermute(other, "ctx", [(c, c - 1) for c in odd])

    *dqs, mine = backward(info, start_rows, q_slots, g_slots, stat, kvs[:1], part=part, delta=delta)
    total = mine + back.astype(F32) + beside.astype(F32) + back_far.astype(F32)
    total = total.astype(BF).reshape(2, n, tok, HD)
    pieces = [
        around(lax.dynamic_index_in_dim(total, lax.rem(x + e, n), 1, keepdims=False), e, n) for e in range(n)
    ]
    dq_parts = [around(dqs[e], -e, n) for e in range(n)]
    pieces, dq_parts = lax.optimization_barrier((pieces, dq_parts))
    ring = jnp.stack(pieces[::-1] + pieces[::-1], axis=0)
    heads = lax.dynamic_slice_in_dim(ring, n - 1 - x, n, 0).transpose(1, 2, 0, 3)

    def whole(parts):
        return unpack(xi, [v.reshape(tok, GROUP, HD) for v in parts])

    return whole(att_parts), whole(dq_parts), heads[0], heads[1]


def solution(mesh):
    spec = P(("ctx", "head"), None, None)
    return jax.shard_map(
        shards,
        mesh=mesh,
        in_specs=(spec, spec, spec, spec, P()),
        out_specs=(spec, spec, spec, spec),
        check_vma=False,
    )
```

```python
import functools
import math

import jax
import jax.numpy as jnp
from jax import lax
from jax.experimental import pallas as pl
from jax.experimental.pallas import tpu as pltpu
from jax.sharding import PartitionSpec as P

HQ = 32
KVH = 4
HD = 128
NBACK = 3
WIN = NBACK + 2
GROUP = HQ // KVH
FACTOR = HD ** -0.5
EXP_SCALE = FACTOR * math.log2(math.e)
NEG = -1e30
FT = 512
HT = 512
PAD = 512
BF = jnp.bfloat16
F32 = jnp.float32
ANY = pl.BlockSpec(memory_space=pl.ANY)
VM = pl.BlockSpec(memory_space=pltpu.VMEM)
SM = pl.BlockSpec(memory_space=pltpu.SMEM)
LIGHT = pl.CostEstimate(flops=1 << 20, bytes_accessed=1 << 21, transcendentals=0)


def params(mb=56):
    return pltpu.CompilerParams(vmem_limit_bytes=mb << 20)


def dot(a, b):
    return lax.dot_general(a, b, (((1,), (0,)), ((), ())), preferred_element_type=F32)

def pack_kernel(n, info, src, *rest):
    outs, sems = rest[:n], rest[n]
    copies = [
        pltpu.make_async_copy(src.at[:, lax.rem(info[0] + e, n)], outs[e], sems.at[e]) for e in range(n)
    ]
    for c in copies:
        c.start()
    for c in copies:
        c.wait()


def pack(info, arr, n):
    tok = arr.shape[0]
    return pl.pallas_call(
        functools.partial(pack_kernel, n),
        in_specs=[SM, VM],
        out_specs=[ANY] * n,
        out_shape=[jax.ShapeDtypeStruct((tok, GROUP, HD), BF)] * n,
        scratch_shapes=[pltpu.SemaphoreType.DMA((n,))],
        cost_estimate=LIGHT,
        name="pack",
    )(info, arr.reshape(tok, n, GROUP, HD))


def unpack_kernel(n, info, *rest):
    srcs, out, sems = rest[:n], rest[n], rest[n + 1]
    copies = [
        pltpu.make_async_copy(srcs[e], out.at[:, lax.rem(info[0] + e, n)], sems.at[e]) for e in range(n)
    ]
    for c in copies:
        c.start()
    for c in copies:
        c.wait()


def unpack(info, parts):
    n = len(parts)
    tok = parts[0].shape[0]
    return pl.pallas_call(
        functools.partial(unpack_kernel, n),
        in_specs=[SM] + [ANY] * n,
        out_specs=VM,
        out_shape=jax.ShapeDtypeStruct((tok, n, GROUP, HD), BF),
        scratch_shapes=[pltpu.SemaphoreType.DMA((n,))],
        cost_estimate=LIGHT,
        name="unpack",
    )(info, *parts).reshape(tok, n * GROUP, HD)


def masked_scores(k, qt, start, pos, base):
    s = dot(k, qt)
    u = base + lax.broadcasted_iota(jnp.int32, s.shape, 0)
    return jnp.where((u >= start) & (u <= pos), s, NEG)


def positions(first, rows):
    return first + lax.broadcasted_iota(jnp.int32, (1, rows), 1) // GROUP


def fwd_kernel(n, shard, info, start_ref, *refs):
    q_in = refs[:n]
    kv_in = refs[n : n + WIN]
    p = n + WIN
    atts = refs[p : p + n]
    stat_out = refs[p + n]
    k_scr, v_scr, vt_scr, acc, q_scr, o_scr, q_sems, o_sems, kv_sems = refs[p + n + 1 :]
    rows = q_scr.shape[1]
    k_in, v_in = [], []
    for w in range(WIN):
        at = pl.ds(PAD + w * shard, shard)
        v_in.append(pltpu.make_async_copy(kv_in[w].at[1], v_scr.at[at], kv_sems.at[2 * w + 1]))
        k_in.append(pltpu.make_async_copy(kv_in[w].at[0], k_scr.at[at], kv_sems.at[2 * w]))
        v_in[w].start()
        k_in[w].start()

    def fetch(e):
        pltpu.make_async_copy(q_in[e], q_scr.at[e], q_sems.at[e]).start()

    fetch(0)
    k_scr[:PAD] = jnp.zeros((PAD, HD), BF)
    vt_scr[:, :PAD] = jnp.zeros((HD, PAD), BF)
    for w in range(WIN):
        at = PAD + w * shard
        v_in[w].wait()
        vt_scr[:, at : at + shard] = v_scr[at : at + shard].T
    for w in range(WIN):
        k_in[w].wait()
    half = rows // 2

    def block(e, carry):
        end = info[2 + e] + rows // GROUP
        steps = (end - info[2 + n + e] + FT - 1) // FT
        start = start_ref[e]
        pos = positions(info[2 + e], rows)
        pltpu.make_async_copy(q_in[0], q_scr.at[e], q_sems.at[e]).wait()
        for f in range(1, n):
            pl.when(e + 1 == f)(functools.partial(fetch, f))
        qt = q_scr[e].T
        acc[...] = jnp.zeros_like(acc)

        def tile(t, state):
            base = end - (t + 1) * FT
            at = pl.multiple_of(base + PAD, 128)
            k = k_scr[pl.ds(at, FT)]
            vt = vt_scr[:, pl.ds(at, FT)]
            ss = [
                masked_scores(k, qt[:, a : a + half], start[:, a : a + half], pos[:, a : a + half], base)
                for a in (0, half)
            ]
            new = []
            for b, s in enumerate(ss):
                m, l = state[b]
                cols = slice(b * half, (b + 1) * half)
                top = jnp.max(jnp.max(s.reshape(FT // 8, 8, half), axis=0), axis=0, keepdims=True)
                m_new = jnp.maximum(m, top)
                fade = jnp.exp2((m - m_new) * EXP_SCALE)
                w = jnp.exp2((s - m_new) * EXP_SCALE)
                acc[:, cols] = acc[:, cols] * fade + dot(vt, w.astype(BF))
                l = l * fade + jnp.sum(w.reshape(FT // 8, 8, half), axis=0)
                new.append((m_new, l))
            return tuple(new)

        first = (jnp.full((1, half), NEG, F32), jnp.zeros((8, half), F32))
        state = lax.fori_loop(0, steps, tile, (first, first))
        m = jnp.concatenate([state[0][0], state[1][0]], axis=1)
        l = jnp.sum(jnp.concatenate([state[0][1], state[1][1]], axis=1), axis=0, keepdims=True)
        o_scr[e] = (acc[...] * (1.0 / l)).astype(BF).T
        stat_out[e] = m * EXP_SCALE + jnp.log2(l)
        for f in range(n):

            @pl.when(e == f)
            def _():
                pltpu.make_async_copy(o_scr.at[f], atts[f], o_sems.at[f]).start()

        return carry

    lax.fori_loop(0, n, block, 0)
    for e in range(n):
        pltpu.make_async_copy(o_scr.at[e], atts[e], o_sems.at[e]).wait()


def forward(info, start, q_slots, kvs):
    n = len(q_slots)
    rows = q_slots[0].shape[0]
    shard = kvs[0].shape[1]
    keys = WIN * shard + PAD
    return pl.pallas_call(
        functools.partial(fwd_kernel, n, shard),
        in_specs=[SM, VM] + [ANY] * (n + WIN),
        out_specs=[ANY] * n + [VM],
        out_shape=[jax.ShapeDtypeStruct((rows, HD), BF)] * n + [jax.ShapeDtypeStruct((n, 1, rows), F32)],
        scratch_shapes=[
            pltpu.VMEM((keys, HD), BF),
            pltpu.VMEM((keys, HD), BF),
            pltpu.VMEM((HD, keys), BF),
            pltpu.VMEM((HD, rows), F32),
            pltpu.VMEM((n, rows, HD), BF),
            pltpu.VMEM((n, rows, HD), BF),
            pltpu.SemaphoreType.DMA((n,)),
            pltpu.SemaphoreType.DMA((n,)),
            pltpu.SemaphoreType.DMA((2 * WIN,)),
        ],
        compiler_params=params(),
        cost_estimate=LIGHT,
        name="forward",
    )(info, start, *q_slots, *kvs)


def bwd_kernel(n, shard, info, start_ref, stat_ref, *refs):
    q_in, g_in, o_in = refs[:n], refs[n : 2 * n], refs[2 * n : 3 * n]
    kv_in = refs[3 * n : 3 * n + WIN]
    p = 3 * n + WIN
    dq_outs = refs[p : p + n]
    own_out, back_out, cross_out, far_out = refs[p + n : p + n + 4]
    p += n + 4
    k_scr, v_scr, kt_scr, dk, dv, acc, q_scr, g_scr, o_scr, p_scr, ds_scr = refs[p : p + 11]
    q_sems, g_sems, o_sems, kv_sems = refs[p + 11 :]
    rows = q_scr.shape[1]
    k_copy, v_copy = [], []
    for w in range(WIN):
        at = pl.ds(PAD + w * shard, shard)
        k_copy.append(pltpu.make_async_copy(kv_in[w].at[0], k_scr.at[at], kv_sems.at[2 * w]))
        v_copy.append(pltpu.make_async_copy(kv_in[w].at[1], v_scr.at[at], kv_sems.at[2 * w + 1]))
        k_copy[w].start()
        v_copy[w].start()

    def fetch(e):
        pltpu.make_async_copy(q_in[e], q_scr.at[e], q_sems.at[e]).start()
        pltpu.make_async_copy(g_in[e], g_scr.at[e], g_sems.at[e]).start()
        pltpu.make_async_copy(o_in[e], o_scr.at[e], o_sems.at[e]).start()

    fetch(0)
    k_scr[:PAD] = jnp.zeros((PAD, HD), BF)
    v_scr[:PAD] = jnp.zeros((PAD, HD), BF)
    kt_scr[:, :PAD] = jnp.zeros((HD, PAD), BF)
    dk[...] = jnp.zeros_like(dk)
    dv[...] = jnp.zeros_like(dv)
    for w in range(WIN):
        at = PAD + w * shard
        k_copy[w].wait()
        kt_scr[:, at : at + shard] = k_scr[at : at + shard].T
    for w in range(WIN):
        v_copy[w].wait()
    half = rows // 2

    def block(e, carry):
        end = info[2 + e] + rows // GROUP
        steps = (end - info[2 + n + e] + HT - 1) // HT
        start = start_ref[e]
        pos = positions(info[2 + e], rows)
        pltpu.make_async_copy(q_in[0], q_scr.at[e], q_sems.at[e]).wait()
        pltpu.make_async_copy(g_in[0], g_scr.at[e], g_sems.at[e]).wait()
        pltpu.make_async_copy(o_in[0], o_scr.at[e], o_sems.at[e]).wait()
        for f in range(1, n):
            pl.when(e + 1 == f)(functools.partial(fetch, f))
        q = q_scr[e]
        g = g_scr[e]
        qt = q.T
        gt = g.T
        acc[...] = jnp.zeros((HD, rows), F32)
        delta = jnp.sum(gt.astype(F32) * o_scr[e].T.astype(F32), axis=0, keepdims=True)
        stat = stat_ref[e]

        def tile(t, c):
            base = end - (t + 1) * HT
            keys = pl.ds(pl.multiple_of(base + PAD, 128), HT)
            k = k_scr[keys]
            v = v_scr[keys]
            for a in (0, half):
                cols = slice(a, a + half)
                s = masked_scores(k, qt[:, cols], start[:, cols], pos[:, cols], base)
                dp = dot(v, gt[:, cols])
                w = jnp.exp2(s * EXP_SCALE - stat[:, cols])
                p_scr[:, cols] = w.astype(BF)
                ds_scr[:, cols] = (w * (dp - delta[:, cols])).astype(BF)
            dv[keys] += dot(p_scr[...], g)
            dk[keys] += dot(ds_scr[...], q)
            acc[...] += dot(kt_scr[:, keys], ds_scr[...])
            return c

        lax.fori_loop(0, steps, tile, 0)
        o_scr[e] = (acc[...] * FACTOR).astype(BF).T
        for f in range(n):

            @pl.when(e == f)
            def _():
                pltpu.make_async_copy(o_scr.at[f], dq_outs[f], o_sems.at[f]).start()

        return carry

    lax.fori_loop(0, n, block, 0)

    def give(ref, w):
        at = PAD + w * shard
        ref[0] = (dk[at : at + shard] * FACTOR).astype(ref.dtype)
        ref[1] = dv[at : at + shard].astype(ref.dtype)

    give(far_out, 0)
    for c in range(2):

        @pl.when(info[1] == c)
        def _():
            give(cross_out.at[0], 4 - c)
            give(cross_out.at[1], 2 - c)
            give(back_out, 1 + c)
            give(own_out, 3 + c)

    for e in range(n):
        pltpu.make_async_copy(o_scr.at[e], dq_outs[e], o_sems.at[e]).wait()


def backward(info, start, q_slots, g_slots, o_slots, stat, kvs):
    n = len(q_slots)
    rows = q_slots[0].shape[0]
    shard = kvs[0].shape[1]
    keys = WIN * shard + PAD
    part = (2, shard, HD)
    return pl.pallas_call(
        functools.partial(bwd_kernel, n, shard),
        in_specs=[SM, VM, VM] + [ANY] * (3 * n + WIN),
        out_specs=[ANY] * n + [VM] * 4,
        out_shape=[jax.ShapeDtypeStruct((rows, HD), BF)] * n
        + [
            jax.ShapeDtypeStruct(part, F32),
            jax.ShapeDtypeStruct(part, F32),
            jax.ShapeDtypeStruct((2,) + part, BF),
            jax.ShapeDtypeStruct(part, BF),
        ],
        scratch_shapes=[
            pltpu.VMEM((keys, HD), BF),
            pltpu.VMEM((keys, HD), BF),
            pltpu.VMEM((HD, keys), BF),
            pltpu.VMEM((keys, HD), F32),
            pltpu.VMEM((keys, HD), F32),
            pltpu.VMEM((HD, rows), F32),
            pltpu.VMEM((n, rows, HD), BF),
            pltpu.VMEM((n, rows, HD), BF),
            pltpu.VMEM((n, rows, HD), BF),
            pltpu.VMEM((HT, rows), BF),
            pltpu.VMEM((HT, rows), BF),
            pltpu.SemaphoreType.DMA((n,)),
            pltpu.SemaphoreType.DMA((n,)),
            pltpu.SemaphoreType.DMA((n,)),
            pltpu.SemaphoreType.DMA((2 * WIN,)),
        ],
        compiler_params=params(),
        cost_estimate=LIGHT,
        name="backward",
    )(info, start, stat, *q_slots, *g_slots, *o_slots, *kvs)


def around(value, shift, n):
    if shift % n == 0:
        return value
    return lax.ppermute(value, "head", [(i, (i + shift) % n) for i in range(n)])


def along(value, steps, starts):
    count = lax.axis_size("ctx")
    pairs = [(c, c + steps) for c in starts if 0 <= c + steps < count]
    return lax.ppermute(value, "ctx", pairs)


def crossing(value, shift, n, home):
    pairs = []
    for c in range(lax.axis_size("ctx")):
        for i in range(n):
            pairs.append((c * n + i, (c ^ (i & 1)) * n + (i + shift) % n))
    if home:
        pairs = [(b, a) for a, b in pairs]
    return lax.ppermute(value, ("ctx", "head"), pairs)


def shards(queries, keys, values, out_grad, doc_ids):
    n = lax.axis_size("head")
    n_ctx = lax.axis_size("ctx")
    tok = queries.shape[0]
    shard = tok * n
    front = NBACK * shard
    x = lax.axis_index("head")
    ctx = lax.axis_index("ctx")
    core = lax.rem(ctx, 2)
    everyone, even, odd = range(n_ctx), range(0, n_ctx, 2), range(1, n_ctx, 2)
    swap = [(c, c ^ 1) for c in everyone]
    first = core == 0
    xi = x[None].astype(jnp.int32)
    order = (2, 1, 3, 0)

    kv = jnp.stack([keys, values]).transpose(2, 0, 1, 3)
    kv_parts = {0: lax.dynamic_index_in_dim(kv, x, 0, keepdims=False)}
    for e in order[:3]:
        kv_parts[e] = around(lax.dynamic_index_in_dim(kv, lax.rem(x + e, n), 0, keepdims=False), e, n)

    def slots(blocks):
        got = {e: crossing(blocks[e], e, n, False) for e in order}
        return [got[e] for e in range(n)]

    def packed(arr):
        return [v.reshape(tok * GROUP, HD) for v in pack(xi, arr, n)]

    q_packed, g_packed = packed(queries), packed(out_grad)
    kv_parts = lax.optimization_barrier((kv_parts, q_packed, g_packed))[0]
    q_slots = slots(q_packed)
    g_slots = slots(g_packed)

    ring = [kv_parts[e] for e in range(n - 1, -1, -1)]
    own = lax.dynamic_slice_in_dim(jnp.concatenate(ring + ring, axis=1), (n - 1 - x) * tok, shard, 1)

    tags_pad = jnp.concatenate([jnp.full((front,), -1, jnp.int32), doc_ids], 0)
    window = lax.dynamic_slice_in_dim(tags_pad, (ctx - core) * shard, WIN * shard, 0)
    places = []
    for e in range(n):
        i = lax.rem(x - e + n, n)
        places.append(front + lax.rem(core + i, 2) * shard + i * tok)
    tags = jnp.concatenate([lax.dynamic_slice_in_dim(window, p, tok, 0) for p in places])
    start = jnp.sum((window[None, :] < tags[:, None]).astype(jnp.int32), axis=1)
    info = jnp.concatenate([jnp.stack([x, core] + places).astype(jnp.int32), start[::tok]])
    start_rows = jnp.repeat(start.reshape(n, 1, tok), GROUP, axis=2)

    behind = along(own, 2, everyone)
    far = along(own, 3, odd)
    own_swap = lax.ppermute(own, "ctx", swap)
    behind_swap = lax.ppermute(behind, "ctx", swap)
    far_swap = lax.ppermute(far, "ctx", [(c, c + 1) for c in even])

    def pick(a, b):
        return jnp.where(first, a, b)

    kvs = [
        pick(far, far_swap),
        pick(behind, behind_swap),
        pick(behind_swap, behind),
        pick(own, own_swap),
        pick(own_swap, own),
    ]

    *atts, stat = forward(info, start_rows, q_slots, kvs)
    att_parts = [crossing(atts[e], e, n, True) for e in range(n)]

    *dqs, mine, straight, cross, part = backward(info, start_rows, q_slots, g_slots, atts, stat, kvs)
    crossed = lax.ppermute(cross, "ctx", swap)
    part_far = lax.ppermute(part, "ctx", [(c, c - 1) for c in odd])
    back = along((straight + crossed[1].astype(F32)).astype(BF), -2, everyone)
    back_far = along((part.astype(F32) + part_far.astype(F32)).astype(BF), -3, even)
    total = mine + crossed[0].astype(F32) + back.astype(F32) + back_far.astype(F32)
    total = total.astype(BF).reshape(2, n, tok, HD)
    pieces = [
        around(lax.dynamic_index_in_dim(total, lax.rem(x + e, n), 1, keepdims=False), e, n) for e in range(n)
    ]
    dq_parts = [crossing(dqs[e], e, n, True) for e in range(n)]
    pieces, dq_parts = lax.optimization_barrier((pieces, dq_parts))
    ring = jnp.stack(pieces[::-1] + pieces[::-1], axis=0)
    heads = lax.dynamic_slice_in_dim(ring, n - 1 - x, n, 0).transpose(1, 2, 0, 3)

    def whole(parts):
        return unpack(xi, [v.reshape(tok, GROUP, HD) for v in parts])

    return whole(att_parts), whole(dq_parts), heads[0], heads[1]


def solution(mesh):
    spec = P(("ctx", "head"), None, None)
    return jax.shard_map(
        shards,
        mesh=mesh,
        in_specs=(spec, spec, spec, spec, P()),
        out_specs=(spec, spec, spec, spec),
        check_vma=False,
    )
```

```python
import functools
import math

import jax
import jax.numpy as jnp
from jax import lax
from jax.experimental import pallas as pl
from jax.experimental.pallas import tpu as pltpu
from jax.sharding import PartitionSpec as P

HQ = 32
KVH = 4
HD = 128
NBACK = 3
WIN = NBACK + 2
GROUP = HQ // KVH
FACTOR = HD ** -0.5
EXP_SCALE = FACTOR * math.log2(math.e)
NEG = -1e30
KT = 512
PAD = 512
BF = jnp.bfloat16
F32 = jnp.float32
ANY = pl.BlockSpec(memory_space=pl.ANY)
VM = pl.BlockSpec(memory_space=pltpu.VMEM)
SM = pl.BlockSpec(memory_space=pltpu.SMEM)
LIGHT = pl.CostEstimate(flops=1 << 20, bytes_accessed=1 << 21, transcendentals=0)
HEAVY = pl.CostEstimate(flops=1 << 35, bytes_accessed=1 << 21, transcendentals=0)


def params(mb=56):
    return pltpu.CompilerParams(vmem_limit_bytes=mb << 20)


def dot(a, b):
    return lax.dot_general(a, b, (((1,), (0,)), ((), ())), preferred_element_type=F32)

def pack_kernel(n, info, q, g, *rest):
    outs, sems = rest[:n], rest[n]
    copies = []
    for e in range(n):
        h = lax.rem(info[0] + e, n)
        copies.append(pltpu.make_async_copy(q.at[:, h], outs[e].at[0], sems.at[0, e]))
        copies.append(pltpu.make_async_copy(g.at[:, h], outs[e].at[1], sems.at[1, e]))
    for c in copies:
        c.start()
    for c in copies:
        c.wait()


def pack(info, q, g, n):
    tok = q.shape[0]
    split = (tok, n, GROUP, HD)
    return pl.pallas_call(
        functools.partial(pack_kernel, n),
        in_specs=[SM, VM, VM],
        out_specs=[ANY] * n,
        out_shape=[jax.ShapeDtypeStruct((2, tok, GROUP, HD), BF)] * n,
        scratch_shapes=[pltpu.SemaphoreType.DMA((2, n))],
        cost_estimate=LIGHT,
        name="pack",
    )(info, q.reshape(split), g.reshape(split))


def unpack_kernel(n, info, *rest):
    srcs, outs, sems = rest[:n], rest[n : n + 2], rest[n + 2]
    copies = []
    for e in range(n):
        h = lax.rem(info[0] + e, n)
        for a in range(2):
            copies.append(pltpu.make_async_copy(srcs[e].at[a], outs[a].at[:, h], sems.at[a, e]))
    for c in copies:
        c.start()
    for c in copies:
        c.wait()


def unpack(info, parts):
    n = len(parts)
    tok = parts[0].shape[1]
    outs = pl.pallas_call(
        functools.partial(unpack_kernel, n),
        in_specs=[SM] + [ANY] * n,
        out_specs=[VM] * 2,
        out_shape=[jax.ShapeDtypeStruct((tok, n, GROUP, HD), BF)] * 2,
        scratch_shapes=[pltpu.SemaphoreType.DMA((2, n))],
        cost_estimate=LIGHT,
        name="unpack",
    )(info, *parts)
    return [o.reshape(tok, n * GROUP, HD) for o in outs]


def masked_scores(k, qt, start, pos, base):
    s = dot(k, qt)
    u = base + lax.broadcasted_iota(jnp.int32, s.shape, 0)
    return jnp.where((u >= start) & (u <= pos), s, NEG)


def attention_kernel(n, shard, group, info, start_ref, *refs):
    last = group == 1
    held = n // 2
    qg_in = refs[:held]
    own, behind, far, own_swap, behind_swap, far_swap = refs[held : held + 6]
    p = held + 6
    if last:
        dk_in, dv_in = refs[p : p + 2]
        p += 2
    res = refs[p : p + held]
    p += held
    if last:
        own_out, back_out, cross_out = refs[p : p + 3]
        p += 3
    else:
        dk_out, dv_out = refs[p : p + 2]
        p += 2
    k_scr, v_scr, kt_scr, vt_scr, dk, dv, acc, x_scr, y_scr, p_scr, ds_scr = refs[p : p + 11]
    x_sems, y_sems, kv_sems, d_sems = refs[p + 11 :]
    rows = x_scr.shape[2]
    half = rows // 2
    found = [
        [far, behind, behind_swap, own, own_swap],
        [far_swap, behind_swap, behind, own_swap, own],
    ]

    def load(w, a, src):
        scr = v_scr if a else k_scr
        at = pl.ds(PAD + w * shard, shard)
        return pltpu.make_async_copy(src.at[a], scr.at[at], kv_sems.at[2 * w + a])

    for c in range(2):

        @pl.when(info[1] == c)
        def _():
            for a in range(2):
                for w in range(WIN):
                    load(w, a, found[c][w]).start()

    def fetch(e):
        pltpu.make_async_copy(qg_in[e], x_scr.at[e], x_sems.at[e]).start()

    fetch(0)
    k_scr[:PAD] = jnp.zeros((PAD, HD), BF)
    v_scr[:PAD] = jnp.zeros((PAD, HD), BF)
    kt_scr[:, :PAD] = jnp.zeros((HD, PAD), BF)
    vt_scr[:, :PAD] = jnp.zeros((HD, PAD), BF)
    if last:
        sums = [pltpu.make_async_copy(i, o, d_sems.at[a]) for a, (i, o) in enumerate(((dk_in, dk), (dv_in, dv)))]
        for c in sums:
            c.start()
    else:
        dk[...] = jnp.zeros_like(dk)
        dv[...] = jnp.zeros_like(dv)
    for a, (scr, tr) in enumerate(((k_scr, kt_scr), (v_scr, vt_scr))):
        for w in range(WIN):
            at = PAD + w * shard
            load(w, a, own).wait()
            tr[:, at : at + shard] = scr[at : at + shard].T
    if last:
        for c in sums:
            c.wait()

    def block(b, carry):
        e = 2 * b + group
        first = info[2 + e]
        end = first + rows // GROUP
        steps = (end - info[2 + n + e] + KT - 1) // KT
        start = start_ref[e]
        pos = first + lax.broadcasted_iota(jnp.int32, (1, rows), 1) // GROUP
        pltpu.make_async_copy(qg_in[0], x_scr.at[b], x_sems.at[b]).wait()
        for f in range(1, held):
            pl.when(b + 1 == f)(functools.partial(fetch, f))
        q = x_scr[b, 0]
        g = x_scr[b, 1]
        qt = q.T
        gt = g.T
        acc[...] = jnp.zeros((HD, rows), F32)

        def keys_of(t):
            base = end - (t + 1) * KT
            return base, pl.ds(pl.multiple_of(base + PAD, 128), KT)

        def forward(t, state):
            base, keys = keys_of(t)
            k = k_scr[keys]
            vt = vt_scr[:, keys]
            ss = [
                masked_scores(k, qt[:, a : a + half], start[:, a : a + half], pos[:, a : a + half], base)
                for a in (0, half)
            ]
            new = []
            for z, s in enumerate(ss):
                m, l = state[z]
                cols = slice(z * half, (z + 1) * half)
                top = jnp.max(jnp.max(s.reshape(KT // 8, 8, half), axis=0), axis=0, keepdims=True)
                m_new = jnp.maximum(m, top)
                fade = jnp.exp2((m - m_new) * EXP_SCALE)
                w = jnp.exp2((s - m_new) * EXP_SCALE)
                acc[:, cols] = acc[:, cols] * fade + dot(vt, w.astype(BF))
                l = l * fade + jnp.sum(w.reshape(KT // 8, 8, half), axis=0)
                new.append((m_new, l))
            return tuple(new)

        none = (jnp.full((1, half), NEG, F32), jnp.zeros((8, half), F32))
        (m0, l0), (m1, l1) = lax.fori_loop(0, steps, forward, (none, none))
        m = jnp.concatenate([m0, m1], axis=1)
        l = jnp.sum(jnp.concatenate([l0, l1], axis=1), axis=0, keepdims=True)
        ot = (acc[...] * (1.0 / l)).astype(BF)
        y_scr[b, 0] = ot.T
        stat = m * EXP_SCALE + jnp.log2(l)
        delta = jnp.sum(gt.astype(F32) * ot.astype(F32), axis=0, keepdims=True)
        acc[...] = jnp.zeros((HD, rows), F32)

        def backward(t, c):
            base, keys = keys_of(t)
            k = k_scr[keys]
            v = v_scr[keys]
            for a in (0, half):
                cols = slice(a, a + half)
                s = masked_scores(k, qt[:, cols], start[:, cols], pos[:, cols], base)
                dp = dot(v, gt[:, cols])
                w = jnp.exp2(s * EXP_SCALE - stat[:, cols])
                p_scr[:, cols] = w.astype(BF)
                ds_scr[:, cols] = (w * (dp - delta[:, cols])).astype(BF)
            dv[keys] += dot(p_scr[...], g)
            dk[keys] += dot(ds_scr[...], q)
            acc[...] += dot(kt_scr[:, keys], ds_scr[...])
            return c

        lax.fori_loop(0, steps, backward, 0)
        y_scr[b, 1] = (acc[...] * FACTOR).astype(BF).T
        for f in range(held):

            @pl.when(b == f)
            def _():
                pltpu.make_async_copy(y_scr.at[f], res[f], y_sems.at[f]).start()

        return carry

    lax.fori_loop(0, held, block, 0)

    def give(ref, w):
        at = PAD + w * shard
        ref[0] = (dk[at : at + shard] * FACTOR).astype(ref.dtype)
        ref[1] = dv[at : at + shard].astype(ref.dtype)

    if last:
        give(cross_out.at[2], 0)
        for c in range(2):

            @pl.when(info[1] == c)
            def _():
                give(cross_out.at[0], 4 - c)
                give(cross_out.at[1], 2 - c)
                give(back_out, 1 + c)
                give(own_out, 3 + c)

    else:
        sums = [pltpu.make_async_copy(i, o, d_sems.at[a]) for a, (i, o) in enumerate(((dk, dk_out), (dv, dv_out)))]
        for c in sums:
            c.start()
        for c in sums:
            c.wait()
    for b in range(held):
        pltpu.make_async_copy(y_scr.at[b], res[b], y_sems.at[b]).wait()


def attention(info, start, group, slots, window, sums=()):
    held = len(slots)
    rows = slots[0].shape[1]
    shard = window[0].shape[1]
    keys = WIN * shard + PAD
    part = (2, shard, HD)
    if group:
        outs = [(part, F32), (part, F32), ((3,) + part, BF)]
        specs = [VM] * 3
    else:
        outs = [((keys, HD), F32)] * 2
        specs = [ANY] * 2
    return pl.pallas_call(
        functools.partial(attention_kernel, 2 * held, shard, group),
        in_specs=[SM, VM] + [ANY] * (held + 6 + len(sums)),
        out_specs=[ANY] * held + specs,
        out_shape=[jax.ShapeDtypeStruct((2, rows, HD), BF)] * held
        + [jax.ShapeDtypeStruct(*o) for o in outs],
        scratch_shapes=[
            pltpu.VMEM((keys, HD), BF),
            pltpu.VMEM((keys, HD), BF),
            pltpu.VMEM((HD, keys), BF),
            pltpu.VMEM((HD, keys), BF),
            pltpu.VMEM((keys, HD), F32),
            pltpu.VMEM((keys, HD), F32),
            pltpu.VMEM((HD, rows), F32),
            pltpu.VMEM((held, 2, rows, HD), BF),
            pltpu.VMEM((held, 2, rows, HD), BF),
            pltpu.VMEM((KT, rows), BF),
            pltpu.VMEM((KT, rows), BF),
            pltpu.SemaphoreType.DMA((held,)),
            pltpu.SemaphoreType.DMA((held,)),
            pltpu.SemaphoreType.DMA((2 * WIN,)),
            pltpu.SemaphoreType.DMA((2,)),
        ],
        compiler_params=params(),
        cost_estimate=LIGHT,
        name="attention_odd" if group else "attention_even",
    )(info, start, *slots, *window, *sums)


def assemble_kernel(n, info, *refs):
    parts, out = refs[:n], refs[n]
    tok = parts[0].shape[1]
    for e in range(n):
        at = pl.multiple_of(lax.rem(info[0] - e + n, n) * tok, tok)
        out[:, pl.ds(at, tok)] = parts[e][...]


def assemble(info, parts):
    n = len(parts)
    _, tok, _ = parts[0].shape
    return pl.pallas_call(
        functools.partial(assemble_kernel, n),
        in_specs=[SM] + [VM] * n,
        out_specs=VM,
        out_shape=jax.ShapeDtypeStruct((2, n * tok, HD), BF),
        cost_estimate=HEAVY,
        name="assemble",
    )(info, *parts)


def join_kernel(mine, straight, cross, crossed, mine_out, back_out, far_out):
    mine_out[...] = mine[...] + crossed[0].astype(F32)
    back_out[...] = (straight[...] + crossed[1].astype(F32)).astype(BF)
    far_out[...] = (cross[2].astype(F32) + crossed[2].astype(F32)).astype(BF)


def join(mine, straight, cross, crossed):
    return pl.pallas_call(
        join_kernel,
        in_specs=[VM] * 4,
        out_specs=[VM] * 3,
        out_shape=[jax.ShapeDtypeStruct(mine.shape, d) for d in (F32, BF, BF)],
        cost_estimate=HEAVY,
        name="join",
    )(mine, straight, cross, crossed)


def around(value, shift, n):
    if shift % n == 0:
        return value
    return lax.ppermute(value, "head", [(i, (i + shift) % n) for i in range(n)])


def along(value, steps, starts):
    count = lax.axis_size("ctx")
    pairs = [(c, c + steps) for c in starts if 0 <= c + steps < count]
    return lax.ppermute(value, "ctx", pairs)


def crossing(value, e, n, home):
    if e == 0:
        return value
    pairs = []
    for c in range(lax.axis_size("ctx")):
        for i in range(n):
            pairs.append((c * n + i, (c ^ (e & 1)) * n + (i + e) % n))
    if home:
        pairs = [(b, a) for a, b in pairs]
    return lax.ppermute(value, ("ctx", "head"), pairs)


def shards(queries, keys, values, out_grad, doc_ids):
    n = lax.axis_size("head")
    n_ctx = lax.axis_size("ctx")
    tok = queries.shape[0]
    shard = tok * n
    front = NBACK * shard
    x = lax.axis_index("head")
    ctx = lax.axis_index("ctx")
    core = lax.rem(ctx, 2)
    everyone, even, odd = range(n_ctx), range(0, n_ctx, 2), range(1, n_ctx, 2)
    swap = [(c, c ^ 1) for c in everyone]
    xi = x[None].astype(jnp.int32)
    order = (2, 1, 3)

    kv = jnp.stack([keys, values]).transpose(2, 0, 1, 3)
    kv_parts = {0: lax.dynamic_index_in_dim(kv, x, 0, keepdims=False)}
    for e in order:
        kv_parts[e] = around(lax.dynamic_index_in_dim(kv, lax.rem(x + e, n), 0, keepdims=False), e, n)

    packed = [v.reshape(2, tok * GROUP, HD) for v in pack(xi, queries, out_grad, n)]
    got = {e: crossing(packed[e], e, n, False) for e in order}
    slots = [packed[0]] + [got[e] for e in range(1, n)]
    kv_parts = lax.optimization_barrier((kv_parts, packed))[0]

    own = assemble(xi, [kv_parts[e] for e in range(n)])
    behind = along(own, 2, everyone)
    far = along(own, 3, odd)
    own_swap, behind_swap, far_swap = [lax.ppermute(v, "ctx", swap) for v in (own, behind, far)]

    tags_pad = jnp.concatenate([jnp.full((front,), -1, jnp.int32), doc_ids], 0)
    window = lax.dynamic_slice_in_dim(tags_pad, (ctx - core) * shard, WIN * shard, 0)
    places = []
    for e in range(n):
        i = lax.rem(x - e + n, n)
        places.append(front + (core if e % 2 == 0 else 1 - core) * shard + i * tok)
    tags = jnp.concatenate([lax.dynamic_slice_in_dim(window, p, tok, 0) for p in places])
    start = jnp.sum((window[None, :] < tags[:, None]).astype(jnp.int32), axis=1)
    info = jnp.concatenate([jnp.stack([x, core] + places).astype(jnp.int32), start[::tok]])
    start_rows = jnp.repeat(start.reshape(n, 1, tok), GROUP, axis=2)

    around_here = (own, behind, far, own_swap, behind_swap, far_swap)
    near, across, *sums = attention(info, start_rows, 0, [slots[0], slots[2]], around_here)
    sent = {2: crossing(across, 2, n, True)}
    right, left, mine, straight, cross = attention(info, start_rows, 1, [slots[1], slots[3]], around_here, sums)
    cross = lax.optimization_barrier((cross, sent))[0]
    crossed = lax.ppermute(cross, "ctx", swap)
    sent[1] = crossing(right, 1, n, True)
    sent[3] = crossing(left, 3, n, True)
    mine, back, back_far = join(mine, straight, cross, crossed)
    back = along(back, -2, everyone)
    back_far = along(back_far, -3, even)
    total = mine + back.astype(F32) + back_far.astype(F32)
    total = total.astype(BF).reshape(2, n, tok, HD)
    pieces = {
        e: around(lax.dynamic_index_in_dim(total, lax.rem(x + e, n), 1, keepdims=False), e, n)
        for e in (0,) + order
    }
    parts = [near] + [sent[e] for e in range(1, n)]
    pieces, parts = lax.optimization_barrier((pieces, parts))
    ring = [pieces[e] for e in range(n - 1, -1, -1)]
    ring = jnp.stack(ring + ring, axis=0)
    heads = lax.dynamic_slice_in_dim(ring, n - 1 - x, n, 0).transpose(1, 2, 0, 3)
    attended, query_grad = unpack(xi, [v.reshape(2, tok, GROUP, HD) for v in parts])
    return attended, query_grad, heads[0], heads[1]


def solution(mesh):
    spec = P(("ctx", "head"), None, None)
    return jax.shard_map(
        shards,
        mesh=mesh,
        in_specs=(spec, spec, spec, spec, P()),
        out_specs=(spec, spec, spec, spec),
        check_vma=False,
    )
```

```python
import functools
import math

import jax
import jax.numpy as jnp
from jax import lax
from jax.experimental import pallas as pl
from jax.experimental.pallas import tpu as pltpu
from jax.sharding import PartitionSpec as P

HQ = 32
KVH = 4
HD = 128
NBACK = 3
WIN = NBACK + 2
GROUP = HQ // KVH
FACTOR = HD ** -0.5
EXP_SCALE = FACTOR * math.log2(math.e)
NEG = -1e30
KT = 512
PAD = 512
BF = jnp.bfloat16
F32 = jnp.float32
ANY = pl.BlockSpec(memory_space=pl.ANY)
VM = pl.BlockSpec(memory_space=pltpu.VMEM)
SM = pl.BlockSpec(memory_space=pltpu.SMEM)
LIGHT = pl.CostEstimate(flops=1 << 20, bytes_accessed=1 << 21, transcendentals=0)
HEAVY = pl.CostEstimate(flops=1 << 35, bytes_accessed=1 << 21, transcendentals=0)


def params(mb=56):
    return pltpu.CompilerParams(vmem_limit_bytes=mb << 20)


def dot(a, b):
    return lax.dot_general(a, b, (((1,), (0,)), ((), ())), preferred_element_type=F32)

def pack_kernel(n, info, q, g, *rest):
    outs, sems = rest[:n], rest[n]
    copies = []
    for e in range(n):
        h = lax.rem(info[0] + e, n)
        copies.append(pltpu.make_async_copy(q.at[:, h], outs[e].at[0], sems.at[0, e]))
        copies.append(pltpu.make_async_copy(g.at[:, h], outs[e].at[1], sems.at[1, e]))
    for c in copies:
        c.start()
    for c in copies:
        c.wait()


def pack(info, q, g, n):
    tok = q.shape[0]
    split = (tok, n, GROUP, HD)
    return pl.pallas_call(
        functools.partial(pack_kernel, n),
        in_specs=[SM, VM, VM],
        out_specs=[ANY] * n,
        out_shape=[jax.ShapeDtypeStruct((2, tok, GROUP, HD), BF)] * n,
        scratch_shapes=[pltpu.SemaphoreType.DMA((2, n))],
        cost_estimate=LIGHT,
        name="pack",
    )(info, q.reshape(split), g.reshape(split))


def unpack_kernel(n, info, *rest):
    srcs, outs, sems = rest[:n], rest[n : n + 2], rest[n + 2]
    copies = []
    for e in range(n):
        h = lax.rem(info[0] + e, n)
        for a in range(2):
            copies.append(pltpu.make_async_copy(srcs[e].at[a], outs[a].at[:, h], sems.at[a, e]))
    for c in copies:
        c.start()
    for c in copies:
        c.wait()


def unpack(info, parts):
    n = len(parts)
    tok = parts[0].shape[1]
    outs = pl.pallas_call(
        functools.partial(unpack_kernel, n),
        in_specs=[SM] + [ANY] * n,
        out_specs=[VM] * 2,
        out_shape=[jax.ShapeDtypeStruct((tok, n, GROUP, HD), BF)] * 2,
        scratch_shapes=[pltpu.SemaphoreType.DMA((2, n))],
        cost_estimate=HEAVY,
        name="unpack",
    )(info, *parts)
    return [o.reshape(tok, n * GROUP, HD) for o in outs]


def masked_scores(k, qt, start, pos, base):
    s = dot(k, qt)
    u = base + lax.broadcasted_iota(jnp.int32, s.shape, 0)
    return jnp.where((u >= start) & (u <= pos), s, NEG)


def attention_kernel(n, shard, group, info, start_ref, *refs):
    last = group == 1
    held = n // 2
    qg_in = refs[:held]
    own, behind, far, own_swap, behind_swap, far_swap = refs[held : held + 6]
    p = held + 6
    if last:
        dk_in, dv_in = refs[p : p + 2]
        p += 2
    res = refs[p : p + held]
    p += held
    if last:
        own_out, back_out, cross_out = refs[p : p + 3]
        p += 3
    else:
        dk_out, dv_out = refs[p : p + 2]
        p += 2
    k_scr, v_scr, kt_scr, vt_scr, dk, dv, acc, x_scr, y_scr, s_scr, p_scr, ds_scr = refs[p : p + 12]
    x_sems, y_sems, kv_sems, d_sems = refs[p + 12 :]
    rows = x_scr.shape[2]
    half = rows // 2
    found = [
        [far, behind, behind_swap, own, own_swap],
        [far_swap, behind_swap, behind, own_swap, own],
    ]

    def load(w, a, src):
        scr = v_scr if a else k_scr
        at = pl.ds(PAD + w * shard, shard)
        return pltpu.make_async_copy(src.at[a], scr.at[at], kv_sems.at[2 * w + a])

    for c in range(2):

        @pl.when(info[1] == c)
        def _():
            for a in range(2):
                for w in range(WIN):
                    load(w, a, found[c][w]).start()

    def fetch(e):
        pltpu.make_async_copy(qg_in[e], x_scr.at[e], x_sems.at[e]).start()

    fetch(0)
    k_scr[:PAD] = jnp.zeros((PAD, HD), BF)
    v_scr[:PAD] = jnp.zeros((PAD, HD), BF)
    kt_scr[:, :PAD] = jnp.zeros((HD, PAD), BF)
    vt_scr[:, :PAD] = jnp.zeros((HD, PAD), BF)
    if last:
        sums = [pltpu.make_async_copy(i, o, d_sems.at[a]) for a, (i, o) in enumerate(((dk_in, dk), (dv_in, dv)))]
        for c in sums:
            c.start()
    else:
        dk[...] = jnp.zeros_like(dk)
        dv[...] = jnp.zeros_like(dv)
    for a, (scr, tr) in enumerate(((k_scr, kt_scr), (v_scr, vt_scr))):
        for w in range(WIN):
            at = PAD + w * shard
            load(w, a, own).wait()
            tr[:, at : at + shard] = scr[at : at + shard].T

    def block(b, carry):
        e = 2 * b + group
        first = info[2 + e]
        end = first + rows // GROUP
        span = end - info[2 + n + e]
        whole = (span + KT // 2 - 1) // KT
        rest = (span > whole * KT).astype(jnp.int32)
        start = start_ref[e]
        pos = first + lax.broadcasted_iota(jnp.int32, (1, rows), 1) // GROUP
        pltpu.make_async_copy(qg_in[0], x_scr.at[b], x_sems.at[b]).wait()
        for f in range(1, held):
            pl.when(b + 1 == f)(functools.partial(fetch, f))
        q = x_scr[b, 0]
        g = x_scr[b, 1]
        qt = q.T
        gt = g.T
        acc[...] = jnp.zeros((HD, rows), F32)

        def keys_of(size, t):
            base = end - t * KT - size
            return base, pl.ds(pl.multiple_of(base + PAD, 128), size)

        def over(tile, state):
            state = lax.fori_loop(0, whole, functools.partial(tile, KT), state)
            return lax.fori_loop(0, rest, lambda _, held: tile(KT // 2, whole, held), state)

        def scores(size, t, m):
            base, keys = keys_of(size, t)
            k = k_scr[keys]
            tops = []
            for a in (0, half):
                cols = slice(a, a + half)
                s = masked_scores(k, qt[:, cols], start[:, cols], pos[:, cols], base)
                s_scr[t, :size, cols] = s
                tops.append(jnp.max(s.reshape(size // 8, 8, half), axis=0))
            return jnp.maximum(m, jnp.concatenate(tops, axis=1))

        m = over(scores, jnp.full((8, rows), NEG, F32))
        m = jnp.max(m, axis=0, keepdims=True) * EXP_SCALE

        def weigh(size, t, l):
            _, keys = keys_of(size, t)
            vt = vt_scr[:, keys]
            sums = []
            for a in (0, half):
                cols = slice(a, a + half)
                w = jnp.exp2(s_scr[t, :size, cols] * EXP_SCALE - m[:, cols])
                acc[:, cols] += dot(vt, w.astype(BF))
                sums.append(jnp.sum(w.reshape(size // 8, 8, half), axis=0))
            return l + jnp.concatenate(sums, axis=1)

        l = over(weigh, jnp.zeros((8, rows), F32))
        l = jnp.sum(l, axis=0, keepdims=True)
        ot = (acc[...] * (1.0 / l)).astype(BF)
        y_scr[b, 0] = ot.T
        stat = m + jnp.log2(l)
        delta = jnp.sum(gt.astype(F32) * ot.astype(F32), axis=0, keepdims=True)
        acc[...] = jnp.zeros((HD, rows), F32)

        def backward(size, t, c):
            _, keys = keys_of(size, t)
            v = v_scr[keys]
            for a in (0, half):
                cols = slice(a, a + half)
                dp = dot(v, gt[:, cols])
                w = jnp.exp2(s_scr[t, :size, cols] * EXP_SCALE - stat[:, cols])
                p_scr[:size, cols] = w.astype(BF)
                ds_scr[:size, cols] = (w * (dp - delta[:, cols])).astype(BF)
            dv[keys] += dot(p_scr[:size], g)
            dk[keys] += dot(ds_scr[:size], q)
            acc[...] += dot(kt_scr[:, keys], ds_scr[:size])
            return c

        if last:

            @pl.when(b == 0)
            def _():
                for c in sums:
                    c.wait()

        over(backward, 0)
        y_scr[b, 1] = (acc[...] * FACTOR).astype(BF).T
        for f in range(held):

            @pl.when(b == f)
            def _():
                pltpu.make_async_copy(y_scr.at[f], res[f], y_sems.at[f]).start()

        return carry

    lax.fori_loop(0, held, block, 0)

    def give(ref, w):
        at = PAD + w * shard
        ref[0] = (dk[at : at + shard] * FACTOR).astype(ref.dtype)
        ref[1] = dv[at : at + shard].astype(ref.dtype)

    if last:
        give(cross_out.at[2], 0)
        for c in range(2):

            @pl.when(info[1] == c)
            def _():
                give(cross_out.at[0], 4 - c)
                give(cross_out.at[1], 2 - c)
                give(back_out, 1 + c)
                give(own_out, 3 + c)

    else:
        sums = [pltpu.make_async_copy(i, o, d_sems.at[a]) for a, (i, o) in enumerate(((dk, dk_out), (dv, dv_out)))]
        for c in sums:
            c.start()
        for c in sums:
            c.wait()
    for b in range(held):
        pltpu.make_async_copy(y_scr.at[b], res[b], y_sems.at[b]).wait()


def attention(info, start, group, slots, window, sums=()):
    held = len(slots)
    rows = slots[0].shape[1]
    shard = window[0].shape[1]
    keys = WIN * shard + PAD
    part = (2, shard, HD)
    if group:
        outs = [(part, F32), (part, F32), ((3,) + part, BF)]
        specs = [VM] * 3
    else:
        outs = [((keys, HD), F32)] * 2
        specs = [ANY] * 2
    return pl.pallas_call(
        functools.partial(attention_kernel, 2 * held, shard, group),
        in_specs=[SM, VM] + [ANY] * (held + 6 + len(sums)),
        out_specs=[ANY] * held + specs,
        out_shape=[jax.ShapeDtypeStruct((2, rows, HD), BF)] * held
        + [jax.ShapeDtypeStruct(*o) for o in outs],
        scratch_shapes=[
            pltpu.VMEM((keys, HD), BF),
            pltpu.VMEM((keys, HD), BF),
            pltpu.VMEM((HD, keys), BF),
            pltpu.VMEM((HD, keys), BF),
            pltpu.VMEM((keys, HD), F32),
            pltpu.VMEM((keys, HD), F32),
            pltpu.VMEM((HD, rows), F32),
            pltpu.VMEM((held, 2, rows, HD), BF),
            pltpu.VMEM((held, 2, rows, HD), BF),
            pltpu.VMEM((WIN - 1, KT, rows), F32),
            pltpu.VMEM((KT, rows), BF),
            pltpu.VMEM((KT, rows), BF),
            pltpu.SemaphoreType.DMA((held,)),
            pltpu.SemaphoreType.DMA((held,)),
            pltpu.SemaphoreType.DMA((2 * WIN,)),
            pltpu.SemaphoreType.DMA((2,)),
        ],
        compiler_params=params(),
        cost_estimate=LIGHT,
        name="attention_odd" if group else "attention_even",
    )(info, start, *slots, *window, *sums)


def around(value, shift, n):
    if shift % n == 0:
        return value
    return lax.ppermute(value, "head", [(i, (i + shift) % n) for i in range(n)])


def along(value, steps, starts):
    count = lax.axis_size("ctx")
    pairs = [(c, c + steps) for c in starts if 0 <= c + steps < count]
    return lax.ppermute(value, "ctx", pairs)


def crossing(value, e, n, home):
    if e == 0:
        return value
    pairs = []
    for c in range(lax.axis_size("ctx")):
        for i in range(n):
            pairs.append((c * n + i, (c ^ (e & 1)) * n + (i + e) % n))
    if home:
        pairs = [(b, a) for a, b in pairs]
    return lax.ppermute(value, ("ctx", "head"), pairs)


def shards(queries, keys, values, out_grad, doc_ids):
    n = lax.axis_size("head")
    n_ctx = lax.axis_size("ctx")
    tok = queries.shape[0]
    shard = tok * n
    front = NBACK * shard
    x = lax.axis_index("head")
    ctx = lax.axis_index("ctx")
    core = lax.rem(ctx, 2)
    everyone, even, odd = range(n_ctx), range(0, n_ctx, 2), range(1, n_ctx, 2)
    swap = [(c, c ^ 1) for c in everyone]
    xi = x[None].astype(jnp.int32)
    order = (2, 1, 3)

    kv = jnp.stack([keys, values]).transpose(2, 0, 1, 3)
    kv_parts = {0: lax.dynamic_index_in_dim(kv, x, 0, keepdims=False)}
    for e in order:
        kv_parts[e] = around(lax.dynamic_index_in_dim(kv, lax.rem(x + e, n), 0, keepdims=False), e, n)

    packed = [v.reshape(2, tok * GROUP, HD) for v in pack(xi, queries, out_grad, n)]
    got = {e: crossing(packed[e], e, n, False) for e in order}
    kv_parts = lax.optimization_barrier((kv_parts, packed))[0]

    ring = [kv_parts[e] for e in range(n - 1, -1, -1)]
    own = lax.dynamic_slice_in_dim(jnp.concatenate(ring + ring, axis=1), (n - 1 - x) * tok, shard, 1)
    behind = along(own, 2, everyone)
    far = along(own, 3, odd)
    own_swap = lax.ppermute(own, "ctx", swap)
    (behind, far), got[2] = lax.optimization_barrier(((behind, far), got[2]))
    behind_swap, far_swap = [lax.ppermute(v, "ctx", swap) for v in (behind, far)]

    tags_pad = jnp.concatenate([jnp.full((front,), -1, jnp.int32), doc_ids], 0)
    window = lax.dynamic_slice_in_dim(tags_pad, (ctx - core) * shard, WIN * shard, 0)
    places = []
    for e in range(n):
        i = lax.rem(x - e + n, n)
        places.append(front + (core if e % 2 == 0 else 1 - core) * shard + i * tok)
    tags = jnp.concatenate([lax.dynamic_slice_in_dim(window, p, tok, 0) for p in places])
    start = jnp.sum((window[None, :] < tags[:, None]).astype(jnp.int32), axis=1)
    info = jnp.concatenate([jnp.stack([x, core] + places).astype(jnp.int32), start[::tok]])
    start_rows = jnp.repeat(start.reshape(n, 1, tok), GROUP, axis=2)

    slots = [packed[0]] + [got[e] for e in range(1, n)]
    around_here = (own, behind, far, own_swap, behind_swap, far_swap)
    near, across, *sums = attention(info, start_rows, 0, [slots[0], slots[2]], around_here)
    sent = {2: crossing(across, 2, n, True)}
    right, left, mine, straight, cross = attention(info, start_rows, 1, [slots[1], slots[3]], around_here, sums)
    cross = lax.optimization_barrier((cross, sent))[0]
    crossed = lax.ppermute(cross, "ctx", swap)
    sent[1] = crossing(right, 1, n, True)
    sent[3] = crossing(left, 3, n, True)
    back = along((straight + crossed[1].astype(F32)).astype(BF), -2, everyone)
    back_far = along((cross[2].astype(F32) + crossed[2].astype(F32)).astype(BF), -3, even)
    mine = mine + crossed[0].astype(F32)
    total = mine + back.astype(F32) + back_far.astype(F32)
    total = total.astype(BF).reshape(2, n, tok, HD)
    pieces = {
        e: around(lax.dynamic_index_in_dim(total, lax.rem(x + e, n), 1, keepdims=False), e, n)
        for e in (0,) + order
    }
    parts = [near] + [sent[e] for e in range(1, n)]
    xi = lax.optimization_barrier((xi, total))[0]
    ring = [pieces[e] for e in range(n - 1, -1, -1)]
    ring = jnp.stack(ring + ring, axis=0)
    heads = lax.dynamic_slice_in_dim(ring, n - 1 - x, n, 0).transpose(1, 2, 0, 3)
    attended, query_grad = unpack(xi, [v.reshape(2, tok, GROUP, HD) for v in parts])
    return attended, query_grad, heads[0], heads[1]


def solution(mesh):
    spec = P(("ctx", "head"), None, None)
    return jax.shard_map(
        shards,
        mesh=mesh,
        in_specs=(spec, spec, spec, spec, P()),
        out_specs=(spec, spec, spec, spec),
        check_vma=False,
    )
```

```python
import functools
import math

import jax
import jax.numpy as jnp
from jax import lax
from jax.experimental import pallas as pl
from jax.experimental.pallas import tpu as pltpu
from jax.sharding import PartitionSpec as P

HQ = 32
KVH = 4
HD = 128
NBACK = 3
WIN = NBACK + 2
GROUP = HQ // KVH
FACTOR = HD ** -0.5
EXP_SCALE = FACTOR * math.log2(math.e)
NEG = -1e30
KT = 512
PAD = 512
BF = jnp.bfloat16
F32 = jnp.float32
ANY = pl.BlockSpec(memory_space=pl.ANY)
VM = pl.BlockSpec(memory_space=pltpu.VMEM)
SM = pl.BlockSpec(memory_space=pltpu.SMEM)
LIGHT = pl.CostEstimate(flops=1 << 20, bytes_accessed=1 << 21, transcendentals=0)
HEAVY = pl.CostEstimate(flops=1 << 35, bytes_accessed=1 << 21, transcendentals=0)


def params(mb=34):
    return pltpu.CompilerParams(vmem_limit_bytes=mb << 20)


def dot(a, b):
    return lax.dot_general(a, b, (((1,), (0,)), ((), ())), preferred_element_type=F32)

def pack_kernel(n, info, q, g, *rest):
    outs, sems = rest[:n], rest[n]
    copies = []
    for e in range(n):
        h = lax.rem(info[0] + e, n)
        copies.append(pltpu.make_async_copy(q.at[:, h], outs[e].at[0], sems.at[0, e]))
        copies.append(pltpu.make_async_copy(g.at[:, h], outs[e].at[1], sems.at[1, e]))
    for c in copies:
        c.start()
    for c in copies:
        c.wait()


def pack(info, q, g, n):
    tok = q.shape[0]
    split = (tok, n, GROUP, HD)
    return pl.pallas_call(
        functools.partial(pack_kernel, n),
        in_specs=[SM, VM, VM],
        out_specs=[ANY] * n,
        out_shape=[jax.ShapeDtypeStruct((2, tok, GROUP, HD), BF)] * n,
        scratch_shapes=[pltpu.SemaphoreType.DMA((2, n))],
        cost_estimate=LIGHT,
        name="pack",
    )(info, q.reshape(split), g.reshape(split))


def unpack_kernel(n, info, *rest):
    srcs, outs, sems = rest[:n], rest[n : n + 2], rest[n + 2]
    copies = []
    for e in range(n):
        h = lax.rem(info[0] + e, n)
        for a in range(2):
            copies.append(pltpu.make_async_copy(srcs[e].at[a], outs[a].at[:, h], sems.at[a, e]))
    for c in copies:
        c.start()
    for c in copies:
        c.wait()


def unpack(info, parts):
    n = len(parts)
    tok = parts[0].shape[1]
    outs = pl.pallas_call(
        functools.partial(unpack_kernel, n),
        in_specs=[SM] + [ANY] * n,
        out_specs=[VM] * 2,
        out_shape=[jax.ShapeDtypeStruct((tok, n, GROUP, HD), BF)] * 2,
        scratch_shapes=[pltpu.SemaphoreType.DMA((2, n))],
        cost_estimate=HEAVY,
        name="unpack",
    )(info, *parts)
    return [o.reshape(tok, n * GROUP, HD) for o in outs]


def masked_scores(k, qt, start, pos, base):
    s = dot(k, qt)
    u = base + lax.broadcasted_iota(jnp.int32, s.shape, 0)
    return jnp.where((u >= start) & (u <= pos), s, NEG)


def attention_kernel(n, shard, group, info, start_ref, *refs):
    last = group == 1
    held = n // 2
    qg_in = refs[:held]
    own, behind, far, own_swap, behind_swap, far_swap = refs[held : held + 6]
    p = held + 6
    if last:
        dk_in, dv_in = refs[p : p + 2]
        p += 2
    res = refs[p : p + held]
    p += held
    if last:
        own_out, back_out, cross_out = refs[p : p + 3]
        p += 3
    else:
        dk_out, dv_out = refs[p : p + 2]
        p += 2
    k_scr, v_scr, kt_scr, vt_scr, dk, dv, acc, x_scr, y_scr, s_scr, p_scr, ds_scr = refs[p : p + 12]
    x_sems, y_sems, kv_sems, d_sems = refs[p + 12 :]
    rows = x_scr.shape[2]
    half = rows // 2
    found = [
        [far, behind, behind_swap, own, own_swap],
        [far_swap, behind_swap, behind, own_swap, own],
    ]

    def load(w, a, src):
        scr = v_scr if a else k_scr
        at = pl.ds(PAD + w * shard, shard)
        return pltpu.make_async_copy(src.at[a], scr.at[at], kv_sems.at[2 * w + a])

    for c in range(2):

        @pl.when(info[1] == c)
        def _():
            for a in range(2):
                for w in range(WIN):
                    load(w, a, found[c][w]).start()

    def fetch(e):
        pltpu.make_async_copy(qg_in[e], x_scr.at[e], x_sems.at[e]).start()

    fetch(0)
    k_scr[:PAD] = jnp.zeros((PAD, HD), BF)
    v_scr[:PAD] = jnp.zeros((PAD, HD), BF)
    kt_scr[:, :PAD] = jnp.zeros((HD, PAD), BF)
    vt_scr[:, :PAD] = jnp.zeros((HD, PAD), BF)
    if last:
        sums = [pltpu.make_async_copy(i, o, d_sems.at[a]) for a, (i, o) in enumerate(((dk_in, dk), (dv_in, dv)))]
        for c in sums:
            c.start()
    else:
        dk[...] = jnp.zeros_like(dk)
        dv[...] = jnp.zeros_like(dv)
    for a, (scr, tr) in enumerate(((k_scr, kt_scr), (v_scr, vt_scr))):
        for w in range(WIN):
            at = PAD + w * shard
            load(w, a, own).wait()
            tr[:, at : at + shard] = scr[at : at + shard].T

    def block(b, carry):
        e = 2 * b + group
        first = info[2 + e]
        end = first + rows // GROUP
        span = end - info[2 + n + e]
        whole = (span + KT // 2 - 1) // KT
        rest = (span > whole * KT).astype(jnp.int32)
        start = start_ref[e]
        pos = first + lax.broadcasted_iota(jnp.int32, (1, rows), 1) // GROUP
        pltpu.make_async_copy(qg_in[0], x_scr.at[b], x_sems.at[b]).wait()
        for f in range(1, held):
            pl.when(b + 1 == f)(functools.partial(fetch, f))
        q = x_scr[b, 0]
        g = x_scr[b, 1]
        qt = q.T
        gt = g.T
        acc[...] = jnp.zeros((HD, rows), F32)

        def keys_of(size, t):
            base = end - t * KT - size
            return base, pl.ds(pl.multiple_of(base + PAD, 128), size)

        def over(tile, state):
            state = lax.fori_loop(0, whole, functools.partial(tile, KT), state)
            return lax.fori_loop(0, rest, lambda _, held: tile(KT // 2, whole, held), state)

        def scores(size, t, m):
            base, keys = keys_of(size, t)
            k = k_scr[keys]
            tops = []
            for a in (0, half):
                cols = slice(a, a + half)
                s = masked_scores(k, qt[:, cols], start[:, cols], pos[:, cols], base)
                s_scr[t, :size, cols] = s
                tops.append(jnp.max(s.reshape(size // 8, 8, half), axis=0))
            return jnp.maximum(m, jnp.concatenate(tops, axis=1))

        m = over(scores, jnp.full((8, rows), NEG, F32))
        m = jnp.max(m, axis=0, keepdims=True) * EXP_SCALE

        def weigh(size, t, l):
            _, keys = keys_of(size, t)
            vt = vt_scr[:, keys]
            sums = []
            for a in (0, half):
                cols = slice(a, a + half)
                w = jnp.exp2(s_scr[t, :size, cols] * EXP_SCALE - m[:, cols])
                acc[:, cols] += dot(vt, w.astype(BF))
                sums.append(jnp.sum(w.reshape(size // 8, 8, half), axis=0))
            return l + jnp.concatenate(sums, axis=1)

        l = over(weigh, jnp.zeros((8, rows), F32))
        l = jnp.sum(l, axis=0, keepdims=True)
        ot = (acc[...] * (1.0 / l)).astype(BF)
        y_scr[b, 0] = ot.T
        stat = m + jnp.log2(l)
        delta = jnp.sum(gt.astype(F32) * ot.astype(F32), axis=0, keepdims=True)
        acc[...] = jnp.zeros((HD, rows), F32)

        def backward(size, t, c):
            _, keys = keys_of(size, t)
            v = v_scr[keys]
            for a in (0, half):
                cols = slice(a, a + half)
                dp = dot(v, gt[:, cols])
                w = jnp.exp2(s_scr[t, :size, cols] * EXP_SCALE - stat[:, cols])
                p_scr[:size, cols] = w.astype(BF)
                ds_scr[:size, cols] = (w * (dp - delta[:, cols])).astype(BF)
            dv[keys] += dot(p_scr[:size], g)
            dk[keys] += dot(ds_scr[:size], q)
            acc[...] += dot(kt_scr[:, keys], ds_scr[:size])
            return c

        if last:

            @pl.when(b == 0)
            def _():
                for c in sums:
                    c.wait()

        over(backward, 0)
        y_scr[b, 1] = (acc[...] * FACTOR).astype(BF).T
        for f in range(held):

            @pl.when(b == f)
            def _():
                pltpu.make_async_copy(y_scr.at[f], res[f], y_sems.at[f]).start()

        return carry

    lax.fori_loop(0, held, block, 0)

    def give(ref, w):
        at = PAD + w * shard
        ref[0] = (dk[at : at + shard] * FACTOR).astype(ref.dtype)
        ref[1] = dv[at : at + shard].astype(ref.dtype)

    if last:
        give(cross_out.at[2], 0)
        for c in range(2):

            @pl.when(info[1] == c)
            def _():
                give(cross_out.at[0], 4 - c)
                give(cross_out.at[1], 2 - c)
                give(back_out, 1 + c)
                give(own_out, 3 + c)

    else:
        sums = [pltpu.make_async_copy(i, o, d_sems.at[a]) for a, (i, o) in enumerate(((dk, dk_out), (dv, dv_out)))]
        for c in sums:
            c.start()
        for c in sums:
            c.wait()
    for b in range(held):
        pltpu.make_async_copy(y_scr.at[b], res[b], y_sems.at[b]).wait()


def attention(info, start, group, slots, window, sums=()):
    held = len(slots)
    rows = slots[0].shape[1]
    shard = window[0].shape[1]
    keys = WIN * shard + PAD
    part = (2, shard, HD)
    if group:
        outs = [(part, F32), (part, F32), ((3,) + part, BF)]
        specs = [VM] * 3
    else:
        outs = [((keys, HD), F32)] * 2
        specs = [ANY] * 2
    return pl.pallas_call(
        functools.partial(attention_kernel, 2 * held, shard, group),
        in_specs=[SM, VM] + [ANY] * (held + 6 + len(sums)),
        out_specs=[ANY] * held + specs,
        out_shape=[jax.ShapeDtypeStruct((2, rows, HD), BF)] * held
        + [jax.ShapeDtypeStruct(*o) for o in outs],
        scratch_shapes=[
            pltpu.VMEM((keys, HD), BF),
            pltpu.VMEM((keys, HD), BF),
            pltpu.VMEM((HD, keys), BF),
            pltpu.VMEM((HD, keys), BF),
            pltpu.VMEM((keys, HD), F32),
            pltpu.VMEM((keys, HD), F32),
            pltpu.VMEM((HD, rows), F32),
            pltpu.VMEM((held, 2, rows, HD), BF),
            pltpu.VMEM((held, 2, rows, HD), BF),
            pltpu.VMEM((WIN - 1, KT, rows), F32),
            pltpu.VMEM((KT, rows), BF),
            pltpu.VMEM((KT, rows), BF),
            pltpu.SemaphoreType.DMA((held,)),
            pltpu.SemaphoreType.DMA((held,)),
            pltpu.SemaphoreType.DMA((2 * WIN,)),
            pltpu.SemaphoreType.DMA((2,)),
        ],
        compiler_params=params(),
        cost_estimate=LIGHT,
        name="attention_odd" if group else "attention_even",
    )(info, start, *slots, *window, *sums)


def around(value, shift, n):
    if shift % n == 0:
        return value
    return lax.ppermute(value, "head", [(i, (i + shift) % n) for i in range(n)])


def along(value, steps, starts):
    count = lax.axis_size("ctx")
    pairs = [(c, c + steps) for c in starts if 0 <= c + steps < count]
    return lax.ppermute(value, "ctx", pairs)


def crossing(value, e, n, home):
    if e == 0:
        return value
    pairs = []
    for c in range(lax.axis_size("ctx")):
        for i in range(n):
            pairs.append((c * n + i, (c ^ (e & 1)) * n + (i + e) % n))
    if home:
        pairs = [(b, a) for a, b in pairs]
    return lax.ppermute(value, ("ctx", "head"), pairs)


def shards(queries, keys, values, out_grad, doc_ids):
    n = lax.axis_size("head")
    n_ctx = lax.axis_size("ctx")
    tok = queries.shape[0]
    shard = tok * n
    front = NBACK * shard
    x = lax.axis_index("head")
    ctx = lax.axis_index("ctx")
    core = lax.rem(ctx, 2)
    everyone, even, odd = range(n_ctx), range(0, n_ctx, 2), range(1, n_ctx, 2)
    swap = [(c, c ^ 1) for c in everyone]
    xi = x[None].astype(jnp.int32)
    order = (2, 1, 3)

    kv = jnp.stack([keys, values]).transpose(2, 0, 1, 3)
    kv_parts = {0: lax.dynamic_index_in_dim(kv, x, 0, keepdims=False)}
    for e in order:
        kv_parts[e] = around(lax.dynamic_index_in_dim(kv, lax.rem(x + e, n), 0, keepdims=False), e, n)

    packed = [v.reshape(2, tok * GROUP, HD) for v in pack(xi, queries, out_grad, n)]
    got = {e: crossing(packed[e], e, n, False) for e in order}
    kv_parts = lax.optimization_barrier((kv_parts, packed))[0]

    ring = [kv_parts[e] for e in range(n - 1, -1, -1)]
    own = lax.dynamic_slice_in_dim(jnp.concatenate(ring + ring, axis=1), (n - 1 - x) * tok, shard, 1)
    behind = along(own, 2, everyone)
    far = along(own, 3, odd)
    tags_pad = jnp.concatenate([jnp.full((front,), -1, jnp.int32), doc_ids], 0)
    window = lax.dynamic_slice_in_dim(tags_pad, (ctx - core) * shard, WIN * shard, 0)
    places = []
    for e in range(n):
        i = lax.rem(x - e + n, n)
        places.append(front + (core if e % 2 == 0 else 1 - core) * shard + i * tok)
    tags = jnp.concatenate([lax.dynamic_slice_in_dim(window, p, tok, 0) for p in places])
    start = jnp.sum((window[None, :] < tags[:, None]).astype(jnp.int32), axis=1)
    info = jnp.concatenate([jnp.stack([x, core] + places).astype(jnp.int32), start[::tok]])
    start_rows = jnp.repeat(start.reshape(n, 1, tok), GROUP, axis=2)

    own_swap = lax.ppermute(own, "ctx", swap)
    behind, far, start_rows, info, got[2] = lax.optimization_barrier((behind, far, start_rows, info, got[2]))
    behind_swap, far_swap = [lax.ppermute(v, "ctx", swap) for v in (behind, far)]

    slots = [packed[0]] + [got[e] for e in range(1, n)]
    around_here = (own, behind, far, own_swap, behind_swap, far_swap)
    near, across, *sums = attention(info, start_rows, 0, [slots[0], slots[2]], around_here)
    sent = {2: crossing(across, 2, n, True)}
    right, left, mine, straight, cross = attention(info, start_rows, 1, [slots[1], slots[3]], around_here, sums)
    cross = lax.optimization_barrier((cross, sent))[0]
    crossed = lax.ppermute(cross, "ctx", swap)
    sent[1] = crossing(right, 1, n, True)
    sent[3] = crossing(left, 3, n, True)
    back = along((straight + crossed[1].astype(F32)).astype(BF), -2, everyone)
    back_far = along((cross[2].astype(F32) + crossed[2].astype(F32)).astype(BF), -3, even)
    mine = mine + crossed[0].astype(F32)
    total = mine + back.astype(F32) + back_far.astype(F32)
    total = total.astype(BF).reshape(2, n, tok, HD)
    pieces = {
        e: around(lax.dynamic_index_in_dim(total, lax.rem(x + e, n), 1, keepdims=False), e, n)
        for e in (0,) + order
    }
    parts = [near] + [sent[e] for e in range(1, n)]
    xi = lax.optimization_barrier((xi, total))[0]
    ring = [pieces[e] for e in range(n - 1, -1, -1)]
    ring = jnp.stack(ring + ring, axis=0)
    heads = lax.dynamic_slice_in_dim(ring, n - 1 - x, n, 0).transpose(1, 2, 0, 3)
    attended, query_grad = unpack(xi, [v.reshape(2, tok, GROUP, HD) for v in parts])
    return attended, query_grad, heads[0], heads[1]


def solution(mesh):
    spec = P(("ctx", "head"), None, None)
    return jax.shard_map(
        shards,
        mesh=mesh,
        in_specs=(spec, spec, spec, spec, P()),
        out_specs=(spec, spec, spec, spec),
        check_vma=False,
    )
```

```python
import functools
import math

import jax
import jax.numpy as jnp
from jax import lax
from jax.experimental import pallas as pl
from jax.experimental.pallas import tpu as pltpu
from jax.sharding import PartitionSpec as P

HQ = 32
KVH = 4
HD = 128
NBACK = 3
WIN = NBACK + 2
GROUP = HQ // KVH
FACTOR = HD ** -0.5
EXP_SCALE = FACTOR * math.log2(math.e)
NEG = -1e30
KT = 512
PAD = 512
BF = jnp.bfloat16
F32 = jnp.float32
ANY = pl.BlockSpec(memory_space=pl.ANY)
VM = pl.BlockSpec(memory_space=pltpu.VMEM)
SM = pl.BlockSpec(memory_space=pltpu.SMEM)
LIGHT = pl.CostEstimate(flops=1 << 20, bytes_accessed=1 << 21, transcendentals=0)
HEAVY = pl.CostEstimate(flops=1 << 35, bytes_accessed=1 << 21, transcendentals=0)


def params(mb=34):
    return pltpu.CompilerParams(vmem_limit_bytes=mb << 20)


def dot(a, b):
    return lax.dot_general(a, b, (((1,), (0,)), ((), ())), preferred_element_type=F32)

def pack_kernel(n, info, q, g, *rest):
    outs, sems = rest[:n], rest[n]
    copies = []
    for e in range(n):
        h = lax.rem(info[0] + e, n)
        copies.append(pltpu.make_async_copy(q.at[:, h], outs[e].at[0], sems.at[0, e]))
        copies.append(pltpu.make_async_copy(g.at[:, h], outs[e].at[1], sems.at[1, e]))
    for c in copies:
        c.start()
    for c in copies:
        c.wait()


def pack(info, q, g, n):
    tok = q.shape[0]
    split = (tok, n, GROUP, HD)
    return pl.pallas_call(
        functools.partial(pack_kernel, n),
        in_specs=[SM, VM, VM],
        out_specs=[ANY] * n,
        out_shape=[jax.ShapeDtypeStruct((2, tok, GROUP, HD), BF)] * n,
        scratch_shapes=[pltpu.SemaphoreType.DMA((2, n))],
        cost_estimate=LIGHT,
        name="pack",
    )(info, q.reshape(split), g.reshape(split))


def unpack_kernel(n, info, *rest):
    srcs, outs, sems = rest[:n], rest[n : n + 2], rest[n + 2]
    copies = []
    for e in range(n):
        h = lax.rem(info[0] + e, n)
        for a in range(2):
            copies.append(pltpu.make_async_copy(srcs[e].at[a], outs[a].at[:, h], sems.at[a, e]))
    for c in copies:
        c.start()
    for c in copies:
        c.wait()


def unpack(info, parts):
    n = len(parts)
    tok = parts[0].shape[1]
    outs = pl.pallas_call(
        functools.partial(unpack_kernel, n),
        in_specs=[SM] + [ANY] * n,
        out_specs=[VM] * 2,
        out_shape=[jax.ShapeDtypeStruct((tok, n, GROUP, HD), BF)] * 2,
        scratch_shapes=[pltpu.SemaphoreType.DMA((2, n))],
        cost_estimate=HEAVY,
        name="unpack",
    )(info, *parts)
    return [o.reshape(tok, n * GROUP, HD) for o in outs]


def masked_scores(k, qt, start, pos, base):
    s = dot(k, qt)
    u = base + lax.broadcasted_iota(jnp.int32, s.shape, 0)
    return jnp.where((u >= start) & (u <= pos), s, NEG)


def attention_kernel(n, shard, group, info, start_ref, *refs):
    last = group == 1
    held = n // 2
    qg_in = refs[:held]
    own, behind, far, own_swap, behind_swap, far_swap = refs[held : held + 6]
    p = held + 6
    if last:
        dk_in, dv_in = refs[p : p + 2]
        p += 2
    res = refs[p : p + held]
    p += held
    if last:
        own_out, back_out, cross_out = refs[p : p + 3]
        p += 3
    else:
        dk_out, dv_out = refs[p : p + 2]
        p += 2
    k_scr, v_scr, kt_scr, vt_scr, dk, dv, acc, x_scr, y_scr, s_scr, p_scr, ds_scr = refs[p : p + 12]
    x_sems, y_sems, kv_sems, d_sems = refs[p + 12 :]
    rows = x_scr.shape[2]
    half = rows // 2
    found = [
        [far, behind, behind_swap, own, own_swap],
        [far_swap, behind_swap, behind, own_swap, own],
    ]

    def load(w, a, src):
        scr = v_scr if a else k_scr
        at = pl.ds(PAD + w * shard, shard)
        return pltpu.make_async_copy(src.at[a], scr.at[at], kv_sems.at[2 * w + a])

    for c in range(2):

        @pl.when(info[1] == c)
        def _():
            for a in range(2):
                for w in range(WIN):
                    load(w, a, found[c][w]).start()

    def fetch(e):
        pltpu.make_async_copy(qg_in[e], x_scr.at[e], x_sems.at[e]).start()

    fetch(0)
    k_scr[:PAD] = jnp.zeros((PAD, HD), BF)
    v_scr[:PAD] = jnp.zeros((PAD, HD), BF)
    kt_scr[:, :PAD] = jnp.zeros((HD, PAD), BF)
    vt_scr[:, :PAD] = jnp.zeros((HD, PAD), BF)
    if last:
        sums = [pltpu.make_async_copy(i, o, d_sems.at[a]) for a, (i, o) in enumerate(((dk_in, dk), (dv_in, dv)))]
        for c in sums:
            c.start()
    else:
        dk[...] = jnp.zeros_like(dk)
        dv[...] = jnp.zeros_like(dv)
    for a, (scr, tr) in enumerate(((k_scr, kt_scr), (v_scr, vt_scr))):
        for w in range(WIN):
            at = PAD + w * shard
            load(w, a, own).wait()
            tr[:, at : at + shard] = scr[at : at + shard].T

    def block(b, carry):
        e = 2 * b + group
        first = info[2 + e]
        end = first + rows // GROUP
        span = end - info[2 + n + e]
        whole = (span + KT // 2 - 1) // KT
        rest = (span > whole * KT).astype(jnp.int32)
        start = start_ref[e]
        pos = first + lax.broadcasted_iota(jnp.int32, (1, rows), 1) // GROUP
        pltpu.make_async_copy(qg_in[0], x_scr.at[b], x_sems.at[b]).wait()
        for f in range(1, held):
            pl.when(b + 1 == f)(functools.partial(fetch, f))
        q = x_scr[b, 0]
        g = x_scr[b, 1]
        qt = q.T
        gt = g.T
        acc[...] = jnp.zeros((HD, rows), F32)

        def keys_of(size, t):
            base = end - t * KT - size
            return base, pl.ds(pl.multiple_of(base + PAD, 128), size)

        def over(tile, state):
            state = lax.fori_loop(0, whole, functools.partial(tile, KT), state)
            return lax.fori_loop(0, rest, lambda _, held: tile(KT // 2, whole, held), state)

        def scores(size, t, m):
            base, keys = keys_of(size, t)
            k = k_scr[keys]
            tops = []
            for a in (0, half):
                cols = slice(a, a + half)
                s = masked_scores(k, qt[:, cols], start[:, cols], pos[:, cols], base)
                s_scr[t, :size, cols] = s
                tops.append(jnp.max(s.reshape(size // 8, 8, half), axis=0))
            return jnp.maximum(m, jnp.concatenate(tops, axis=1))

        m = over(scores, jnp.full((8, rows), NEG, F32))
        m = jnp.max(m, axis=0, keepdims=True) * EXP_SCALE

        def weigh(size, t, l):
            _, keys = keys_of(size, t)
            vt = vt_scr[:, keys]
            sums = []
            for a in (0, half):
                cols = slice(a, a + half)
                w = jnp.exp2(s_scr[t, :size, cols] * EXP_SCALE - m[:, cols])
                acc[:, cols] += dot(vt, w.astype(BF))
                sums.append(jnp.sum(w.reshape(size // 8, 8, half), axis=0))
            return l + jnp.concatenate(sums, axis=1)

        l = over(weigh, jnp.zeros((8, rows), F32))
        l = jnp.sum(l, axis=0, keepdims=True)
        ot = (acc[...] * (1.0 / l)).astype(BF)
        y_scr[b, 0] = ot.T
        stat = m + jnp.log2(l)
        delta = jnp.sum(gt.astype(F32) * ot.astype(F32), axis=0, keepdims=True)
        acc[...] = jnp.zeros((HD, rows), F32)

        def backward(size, t, c):
            _, keys = keys_of(size, t)
            v = v_scr[keys]
            for a in (0, half):
                cols = slice(a, a + half)
                dp = dot(v, gt[:, cols])
                w = jnp.exp2(s_scr[t, :size, cols] * EXP_SCALE - stat[:, cols])
                p_scr[:size, cols] = w.astype(BF)
                ds_scr[:size, cols] = (w * (dp - delta[:, cols])).astype(BF)
            dv[keys] += dot(p_scr[:size], g)
            dk[keys] += dot(ds_scr[:size], q)
            acc[...] += dot(kt_scr[:, keys], ds_scr[:size])
            return c

        if last:

            @pl.when(b == 0)
            def _():
                for c in sums:
                    c.wait()

        over(backward, 0)
        y_scr[b, 1] = (acc[...] * FACTOR).astype(BF).T
        for f in range(held):

            @pl.when(b == f)
            def _():
                pltpu.make_async_copy(y_scr.at[f], res[f], y_sems.at[f]).start()

        return carry

    lax.fori_loop(0, held, block, 0)

    def give(ref, w):
        at = PAD + w * shard
        ref[0] = (dk[at : at + shard] * FACTOR).astype(ref.dtype)
        ref[1] = dv[at : at + shard].astype(ref.dtype)

    if last:
        give(cross_out.at[2], 0)
        for c in range(2):

            @pl.when(info[1] == c)
            def _():
                give(cross_out.at[0], 4 - c)
                give(cross_out.at[1], 2 - c)
                give(back_out, 1 + c)
                give(own_out, 3 + c)

    else:
        sums = [pltpu.make_async_copy(i, o, d_sems.at[a]) for a, (i, o) in enumerate(((dk, dk_out), (dv, dv_out)))]
        for c in sums:
            c.start()
        for c in sums:
            c.wait()
    for b in range(held):
        pltpu.make_async_copy(y_scr.at[b], res[b], y_sems.at[b]).wait()


def attention(info, start, group, slots, window, sums=()):
    held = len(slots)
    rows = slots[0].shape[1]
    shard = window[0].shape[1]
    keys = WIN * shard + PAD
    part = (2, shard, HD)
    if group:
        outs = [(part, F32), (part, F32), ((3,) + part, BF)]
        specs = [VM] * 3
    else:
        outs = [((keys, HD), F32)] * 2
        specs = [ANY] * 2
    return pl.pallas_call(
        functools.partial(attention_kernel, 2 * held, shard, group),
        in_specs=[SM, VM] + [ANY] * (held + 6 + len(sums)),
        out_specs=[ANY] * held + specs,
        out_shape=[jax.ShapeDtypeStruct((2, rows, HD), BF)] * held
        + [jax.ShapeDtypeStruct(*o) for o in outs],
        scratch_shapes=[
            pltpu.VMEM((keys, HD), BF),
            pltpu.VMEM((keys, HD), BF),
            pltpu.VMEM((HD, keys), BF),
            pltpu.VMEM((HD, keys), BF),
            pltpu.VMEM((keys, HD), F32),
            pltpu.VMEM((keys, HD), F32),
            pltpu.VMEM((HD, rows), F32),
            pltpu.VMEM((held, 2, rows, HD), BF),
            pltpu.VMEM((held, 2, rows, HD), BF),
            pltpu.VMEM((WIN - 1, KT, rows), F32),
            pltpu.VMEM((KT, rows), BF),
            pltpu.VMEM((KT, rows), BF),
            pltpu.SemaphoreType.DMA((held,)),
            pltpu.SemaphoreType.DMA((held,)),
            pltpu.SemaphoreType.DMA((2 * WIN,)),
            pltpu.SemaphoreType.DMA((2,)),
        ],
        compiler_params=params(),
        cost_estimate=LIGHT,
        name="attention_odd" if group else "attention_even",
    )(info, start, *slots, *window, *sums)


def around(value, shift, n):
    if shift % n == 0:
        return value
    return lax.ppermute(value, "head", [(i, (i + shift) % n) for i in range(n)])


def along(value, steps, starts):
    count = lax.axis_size("ctx")
    pairs = [(c, c + steps) for c in starts if 0 <= c + steps < count]
    return lax.ppermute(value, "ctx", pairs)


def crossing(value, e, n, home):
    if e == 0:
        return value
    pairs = []
    for c in range(lax.axis_size("ctx")):
        for i in range(n):
            pairs.append((c * n + i, (c ^ (e & 1)) * n + (i + e) % n))
    if home:
        pairs = [(b, a) for a, b in pairs]
    return lax.ppermute(value, ("ctx", "head"), pairs)


def shards(queries, keys, values, out_grad, doc_ids):
    n = lax.axis_size("head")
    n_ctx = lax.axis_size("ctx")
    tok = queries.shape[0]
    shard = tok * n
    front = NBACK * shard
    x = lax.axis_index("head")
    ctx = lax.axis_index("ctx")
    core = lax.rem(ctx, 2)
    everyone, even, odd = range(n_ctx), range(0, n_ctx, 2), range(1, n_ctx, 2)
    swap = [(c, c ^ 1) for c in everyone]
    xi = x[None].astype(jnp.int32)
    order = (2, 1, 3)

    kv = jnp.stack([keys, values]).transpose(2, 0, 1, 3)
    kv_parts = {0: lax.dynamic_index_in_dim(kv, x, 0, keepdims=False)}
    for e in order:
        kv_parts[e] = around(lax.dynamic_index_in_dim(kv, lax.rem(x + e, n), 0, keepdims=False), e, n)

    packed = [v.reshape(2, tok * GROUP, HD) for v in pack(xi, queries, out_grad, n)]
    got = {e: crossing(packed[e], e, n, False) for e in order}
    kv_parts = lax.optimization_barrier((kv_parts, packed))[0]

    ring = [kv_parts[e] for e in range(n - 1, -1, -1)]
    own = lax.dynamic_slice_in_dim(jnp.concatenate(ring + ring, axis=1), (n - 1 - x) * tok, shard, 1)
    behind = along(own, 2, everyone)
    far = along(own, 3, odd)
    tags_pad = jnp.concatenate([jnp.full((front,), -1, jnp.int32), doc_ids], 0)
    window = lax.dynamic_slice_in_dim(tags_pad, (ctx - core) * shard, WIN * shard, 0)
    places = []
    for e in range(n):
        i = lax.rem(x - e + n, n)
        places.append(front + (core if e % 2 == 0 else 1 - core) * shard + i * tok)
    tags = jnp.concatenate([lax.dynamic_slice_in_dim(window, p, tok, 0) for p in places])
    start = jnp.sum((window[None, :] < tags[:, None]).astype(jnp.int32), axis=1)
    info = jnp.concatenate([jnp.stack([x, core] + places).astype(jnp.int32), start[::tok]])
    start_rows = jnp.repeat(start.reshape(n, 1, tok), GROUP, axis=2)

    own_swap = lax.ppermute(own, "ctx", swap)
    behind, far, start_rows, info, got[2] = lax.optimization_barrier((behind, far, start_rows, info, got[2]))
    behind_swap, far_swap = [lax.ppermute(v, "ctx", swap) for v in (behind, far)]

    slots = [packed[0]] + [got[e] for e in range(1, n)]
    around_here = (own, behind, far, own_swap, behind_swap, far_swap)
    near, across, *sums = attention(info, start_rows, 0, [slots[0], slots[2]], around_here)
    sent = {2: crossing(across, 2, n, True)}
    right, left, mine, straight, cross = attention(info, start_rows, 1, [slots[1], slots[3]], around_here, sums)
    cross = lax.optimization_barrier((cross, sent))[0]
    crossed = lax.ppermute(cross, "ctx", swap)
    sent[1] = crossing(right, 1, n, True)
    sent[3] = crossing(left, 3, n, True)
    back = along((straight + crossed[1].astype(F32)).astype(BF), -2, everyone)
    back_far = along((cross[2].astype(F32) + crossed[2].astype(F32)).astype(BF), -3, even)
    mine, sent = lax.optimization_barrier((mine + crossed[0].astype(F32), sent))
    total = mine + back.astype(F32) + back_far.astype(F32)
    total = total.astype(BF).reshape(2, n, tok, HD)
    pieces = {
        e: around(lax.dynamic_index_in_dim(total, lax.rem(x + e, n), 1, keepdims=False), e, n)
        for e in (0,) + order
    }
    parts = [near] + [sent[e] for e in range(1, n)]
    xi = lax.optimization_barrier((xi, total))[0]
    ring = [pieces[e] for e in range(n - 1, -1, -1)]
    ring = jnp.stack(ring + ring, axis=0)
    heads = lax.dynamic_slice_in_dim(ring, n - 1 - x, n, 0).transpose(1, 2, 0, 3)
    attended, query_grad = unpack(xi, [v.reshape(2, tok, GROUP, HD) for v in parts])
    return attended, query_grad, heads[0], heads[1]


def solution(mesh):
    spec = P(("ctx", "head"), None, None)
    return jax.shard_map(
        shards,
        mesh=mesh,
        in_specs=(spec, spec, spec, spec, P()),
        out_specs=(spec, spec, spec, spec),
        check_vma=False,
    )
```

```python
import functools
import math

import jax
import jax.numpy as jnp
from jax import lax
from jax.experimental import pallas as pl
from jax.experimental.pallas import tpu as pltpu
from jax.sharding import PartitionSpec as P

HQ = 32
KVH = 4
HD = 128
NBACK = 3
WIN = NBACK + 2
GROUP = HQ // KVH
FACTOR = HD ** -0.5
EXP_SCALE = FACTOR * math.log2(math.e)
NEG = -1e30
KT = 512
PAD = 512
BF = jnp.bfloat16
F32 = jnp.float32
ANY = pl.BlockSpec(memory_space=pl.ANY)
VM = pl.BlockSpec(memory_space=pltpu.VMEM)
SM = pl.BlockSpec(memory_space=pltpu.SMEM)
LIGHT = pl.CostEstimate(flops=1 << 20, bytes_accessed=1 << 21, transcendentals=0)
HEAVY = pl.CostEstimate(flops=1 << 35, bytes_accessed=1 << 21, transcendentals=0)


def params(mb=34):
    return pltpu.CompilerParams(vmem_limit_bytes=mb << 20)


def dot(a, b):
    return lax.dot_general(a, b, (((1,), (0,)), ((), ())), preferred_element_type=F32)

def pack_kernel(n, info, q, g, *rest):
    outs, (scr, in_sems, sems) = rest[:n], rest[n:]
    reads = [pltpu.make_async_copy(src, scr.at[a], in_sems.at[a]) for a, src in enumerate((q, g))]
    for c in reads:
        c.start()
    copies = []
    for a in range(2):
        reads[a].wait()
        for e in range(n):
            h = lax.rem(info[0] + e, n)
            copies.append(pltpu.make_async_copy(scr.at[a, :, h], outs[e].at[a], sems.at[a, e]))
            copies[-1].start()
    for c in copies:
        c.wait()


def pack(info, q, g, n):
    tok = q.shape[0]
    split = (tok, n, GROUP, HD)
    return pl.pallas_call(
        functools.partial(pack_kernel, n),
        in_specs=[SM, ANY, ANY],
        out_specs=[ANY] * n,
        out_shape=[jax.ShapeDtypeStruct((2, tok, GROUP, HD), BF)] * n,
        scratch_shapes=[
            pltpu.VMEM((2,) + split, BF),
            pltpu.SemaphoreType.DMA((2,)),
            pltpu.SemaphoreType.DMA((2, n)),
        ],
        cost_estimate=LIGHT,
        name="pack",
    )(info, q.reshape(split), g.reshape(split))


def unpack_kernel(n, info, *rest):
    srcs, outs, (scr, sems, out_sems) = rest[:n], rest[n : n + 2], rest[n + 2 :]
    reads, writes = [], []
    for a in range(2):
        for e in range(n):
            h = lax.rem(info[0] + e, n)
            reads.append(pltpu.make_async_copy(srcs[e].at[a], scr.at[a, :, h], sems.at[a, e]))
            reads[-1].start()
    for a in range(2):
        for e in range(n):
            reads[a * n + e].wait()
        writes.append(pltpu.make_async_copy(scr.at[a], outs[a], out_sems.at[a]))
        writes[a].start()
    for c in writes:
        c.wait()


def unpack(info, parts):
    n = len(parts)
    tok = parts[0].shape[1]
    split = (tok, n, GROUP, HD)
    outs = pl.pallas_call(
        functools.partial(unpack_kernel, n),
        in_specs=[SM] + [ANY] * n,
        out_specs=[ANY] * 2,
        out_shape=[jax.ShapeDtypeStruct(split, BF)] * 2,
        scratch_shapes=[
            pltpu.VMEM((2,) + split, BF),
            pltpu.SemaphoreType.DMA((2, n)),
            pltpu.SemaphoreType.DMA((2,)),
        ],
        cost_estimate=HEAVY,
        name="unpack",
    )(info, *parts)
    return [o.reshape(tok, n * GROUP, HD) for o in outs]


def masked_scores(k, qt, start, pos, base):
    s = dot(k, qt)
    u = base + lax.broadcasted_iota(jnp.int32, s.shape, 0)
    return jnp.where((u >= start) & (u <= pos), s, NEG)


def attention_kernel(n, shard, group, info, start_ref, *refs):
    last = group == 1
    held = n // 2
    qg_in = refs[:held]
    own, behind, far, own_swap, behind_swap, far_swap = refs[held : held + 6]
    p = held + 6
    if last:
        dk_in, dv_in = refs[p : p + 2]
        p += 2
    res = refs[p : p + held]
    p += held
    if last:
        own_out, back_out, cross_out = refs[p : p + 3]
        p += 3
    else:
        dk_out, dv_out = refs[p : p + 2]
        p += 2
    k_scr, v_scr, kt_scr, vt_scr, dk, dv, acc, x_scr, y_scr, s_scr, p_scr, ds_scr = refs[p : p + 12]
    x_sems, y_sems, kv_sems, d_sems = refs[p + 12 :]
    rows = x_scr.shape[2]
    half = rows // 2
    found = [
        [far, behind, behind_swap, own, own_swap],
        [far_swap, behind_swap, behind, own_swap, own],
    ]

    def load(w, a, src):
        scr = v_scr if a else k_scr
        at = pl.ds(PAD + w * shard, shard)
        return pltpu.make_async_copy(src.at[a], scr.at[at], kv_sems.at[2 * w + a])

    def fetch(e):
        pltpu.make_async_copy(qg_in[e], x_scr.at[e], x_sems.at[e]).start()

    for a in range(2):
        for c in range(2):

            @pl.when(info[1] == c)
            def _():
                for w in range(WIN):
                    load(w, a, found[c][w]).start()

        if a == 0:
            fetch(0)
    k_scr[:PAD] = jnp.zeros((PAD, HD), BF)
    v_scr[:PAD] = jnp.zeros((PAD, HD), BF)
    kt_scr[:, :PAD] = jnp.zeros((HD, PAD), BF)
    vt_scr[:, :PAD] = jnp.zeros((HD, PAD), BF)
    if last:
        body = pl.ds(PAD, WIN * shard)
        sums = [
            pltpu.make_async_copy(i, o.at[body], d_sems.at[a])
            for a, (i, o) in enumerate(((dk_in, dk), (dv_in, dv)))
        ]
        for c in sums:
            c.start()
        dk[:PAD] = jnp.zeros((PAD, HD), F32)
        dv[:PAD] = jnp.zeros((PAD, HD), F32)
    else:
        dk[...] = jnp.zeros_like(dk)
        dv[...] = jnp.zeros_like(dv)

    def arrive(a, scr, tr):
        for w in range(WIN):
            at = PAD + w * shard
            load(w, a, own).wait()
            tr[:, at : at + shard] = scr[at : at + shard].T

    arrive(0, k_scr, kt_scr)

    def block(b, carry):
        e = 2 * b + group
        first = info[2 + e]
        end = first + rows // GROUP
        span = end - info[2 + n + e]
        whole = (span + KT // 2 - 1) // KT
        rest = (span > whole * KT).astype(jnp.int32)
        start = start_ref[e]
        pos = first + lax.broadcasted_iota(jnp.int32, (1, rows), 1) // GROUP
        pltpu.make_async_copy(qg_in[0], x_scr.at[b], x_sems.at[b]).wait()
        for f in range(1, held):
            pl.when(b + 1 == f)(functools.partial(fetch, f))
        q = x_scr[b, 0]
        g = x_scr[b, 1]
        qt = q.T
        gt = g.T
        acc[...] = jnp.zeros((HD, rows), F32)

        def keys_of(size, t):
            base = end - t * KT - size
            return base, pl.ds(pl.multiple_of(base + PAD, 128), size)

        def over(tile, state):
            state = lax.fori_loop(0, whole, functools.partial(tile, KT), state)
            return lax.fori_loop(0, rest, lambda _, held: tile(KT // 2, whole, held), state)

        def scores(size, t, m):
            base, keys = keys_of(size, t)
            k = k_scr[keys]
            tops = []
            for a in (0, half):
                cols = slice(a, a + half)
                s = masked_scores(k, qt[:, cols], start[:, cols], pos[:, cols], base)
                s_scr[t, :size, cols] = s
                tops.append(jnp.max(s.reshape(size // 8, 8, half), axis=0))
            return jnp.maximum(m, jnp.concatenate(tops, axis=1))

        m = over(scores, jnp.full((8, rows), NEG, F32))
        m = jnp.max(m, axis=0, keepdims=True) * EXP_SCALE

        pl.when(b == 0)(functools.partial(arrive, 1, v_scr, vt_scr))

        def weigh(size, t, l):
            _, keys = keys_of(size, t)
            vt = vt_scr[:, keys]
            sums = []
            for a in (0, half):
                cols = slice(a, a + half)
                w = jnp.exp2(s_scr[t, :size, cols] * EXP_SCALE - m[:, cols])
                acc[:, cols] += dot(vt, w.astype(BF))
                sums.append(jnp.sum(w.reshape(size // 8, 8, half), axis=0))
            return l + jnp.concatenate(sums, axis=1)

        l = over(weigh, jnp.zeros((8, rows), F32))
        l = jnp.sum(l, axis=0, keepdims=True)
        ot = (acc[...] * (1.0 / l)).astype(BF)
        y_scr[b, 0] = ot.T
        stat = m + jnp.log2(l)
        delta = jnp.sum(gt.astype(F32) * ot.astype(F32), axis=0, keepdims=True)
        acc[...] = jnp.zeros((HD, rows), F32)

        def backward(size, t, c):
            _, keys = keys_of(size, t)
            v = v_scr[keys]
            for a in (0, half):
                cols = slice(a, a + half)
                dp = dot(v, gt[:, cols])
                w = jnp.exp2(s_scr[t, :size, cols] * EXP_SCALE - stat[:, cols])
                p_scr[:size, cols] = w.astype(BF)
                ds_scr[:size, cols] = (w * (dp - delta[:, cols])).astype(BF)
            dv[keys] += dot(p_scr[:size], g)
            dk[keys] += dot(ds_scr[:size], q)
            acc[...] += dot(kt_scr[:, keys], ds_scr[:size])
            return c

        if last:

            @pl.when(b == 0)
            def _():
                for c in sums:
                    c.wait()

        over(backward, 0)
        y_scr[b, 1] = (acc[...] * FACTOR).astype(BF).T
        for f in range(held):

            @pl.when(b == f)
            def _():
                pltpu.make_async_copy(y_scr.at[f], res[f], y_sems.at[f]).start()

        return carry

    lax.fori_loop(0, held, block, 0)

    def give(ref, w):
        at = PAD + w * shard
        ref[0] = (dk[at : at + shard] * FACTOR).astype(ref.dtype)
        ref[1] = dv[at : at + shard].astype(ref.dtype)

    if last:
        give(cross_out.at[2], 0)
        for c in range(2):

            @pl.when(info[1] == c)
            def _():
                give(cross_out.at[0], 4 - c)
                give(cross_out.at[1], 2 - c)
                give(back_out, 1 + c)
                give(own_out, 3 + c)

    else:
        body = pl.ds(PAD, WIN * shard)
        sums = [
            pltpu.make_async_copy(i.at[body], o, d_sems.at[a])
            for a, (i, o) in enumerate(((dk, dk_out), (dv, dv_out)))
        ]
        for c in sums:
            c.start()
        for c in sums:
            c.wait()
    for b in range(held):
        pltpu.make_async_copy(y_scr.at[b], res[b], y_sems.at[b]).wait()


def attention(info, start, group, slots, window, sums=()):
    held = len(slots)
    rows = slots[0].shape[1]
    shard = window[0].shape[1]
    keys = WIN * shard + PAD
    part = (2, shard, HD)
    if group:
        outs = [(part, F32), (part, F32), ((3,) + part, BF)]
        specs = [VM] * 3
    else:
        outs = [((WIN * shard, HD), F32)] * 2
        specs = [ANY] * 2
    return pl.pallas_call(
        functools.partial(attention_kernel, 2 * held, shard, group),
        in_specs=[SM, VM] + [ANY] * (held + 6 + len(sums)),
        out_specs=[ANY] * held + specs,
        out_shape=[jax.ShapeDtypeStruct((2, rows, HD), BF)] * held
        + [jax.ShapeDtypeStruct(*o) for o in outs],
        scratch_shapes=[
            pltpu.VMEM((keys, HD), BF),
            pltpu.VMEM((keys, HD), BF),
            pltpu.VMEM((HD, keys), BF),
            pltpu.VMEM((HD, keys), BF),
            pltpu.VMEM((keys, HD), F32),
            pltpu.VMEM((keys, HD), F32),
            pltpu.VMEM((HD, rows), F32),
            pltpu.VMEM((held, 2, rows, HD), BF),
            pltpu.VMEM((held, 2, rows, HD), BF),
            pltpu.VMEM((WIN - 1, KT, rows), F32),
            pltpu.VMEM((KT, rows), BF),
            pltpu.VMEM((KT, rows), BF),
            pltpu.SemaphoreType.DMA((held,)),
            pltpu.SemaphoreType.DMA((held,)),
            pltpu.SemaphoreType.DMA((2 * WIN,)),
            pltpu.SemaphoreType.DMA((2,)),
        ],
        compiler_params=params(),
        cost_estimate=LIGHT,
        name="attention_odd" if group else "attention_even",
    )(info, start, *slots, *window, *sums)


def around(value, shift, n):
    if shift % n == 0:
        return value
    return lax.ppermute(value, "head", [(i, (i + shift) % n) for i in range(n)])


def along(value, steps, starts):
    count = lax.axis_size("ctx")
    pairs = [(c, c + steps) for c in starts if 0 <= c + steps < count]
    return lax.ppermute(value, "ctx", pairs)


def crossing(value, e, n, home):
    if e == 0:
        return value
    pairs = []
    for c in range(lax.axis_size("ctx")):
        for i in range(n):
            pairs.append((c * n + i, (c ^ (e & 1)) * n + (i + e) % n))
    if home:
        pairs = [(b, a) for a, b in pairs]
    return lax.ppermute(value, ("ctx", "head"), pairs)


def shards(queries, keys, values, out_grad, doc_ids):
    n = lax.axis_size("head")
    n_ctx = lax.axis_size("ctx")
    tok = queries.shape[0]
    shard = tok * n
    front = NBACK * shard
    x = lax.axis_index("head")
    ctx = lax.axis_index("ctx")
    core = lax.rem(ctx, 2)
    everyone, even, odd = range(n_ctx), range(0, n_ctx, 2), range(1, n_ctx, 2)
    swap = [(c, c ^ 1) for c in everyone]
    xi = x[None].astype(jnp.int32)
    order = (2, 1, 3)

    kv = jnp.stack([keys, values]).transpose(2, 0, 1, 3)
    kv_parts = {0: lax.dynamic_index_in_dim(kv, x, 0, keepdims=False)}
    for e in order:
        kv_parts[e] = around(lax.dynamic_index_in_dim(kv, lax.rem(x + e, n), 0, keepdims=False), e, n)

    packed = [v.reshape(2, tok * GROUP, HD) for v in pack(xi, queries, out_grad, n)]
    got = {e: crossing(packed[e], e, n, False) for e in order}
    kv_parts = lax.optimization_barrier((kv_parts, packed))[0]

    ring = [kv_parts[e] for e in range(n - 1, -1, -1)]
    own = lax.dynamic_slice_in_dim(jnp.concatenate(ring + ring, axis=1), (n - 1 - x) * tok, shard, 1)
    behind = along(own, 2, everyone)
    far = along(own, 3, odd)
    tags_pad = jnp.concatenate([jnp.full((front,), -1, jnp.int32), doc_ids], 0)
    window = lax.dynamic_slice_in_dim(tags_pad, (ctx - core) * shard, WIN * shard, 0)
    places = []
    for e in range(n):
        i = lax.rem(x - e + n, n)
        places.append(front + (core if e % 2 == 0 else 1 - core) * shard + i * tok)
    tags = jnp.concatenate([lax.dynamic_slice_in_dim(window, p, tok, 0) for p in places])
    start = jnp.sum((window[None, :] < tags[:, None]).astype(jnp.int32), axis=1)
    info = jnp.concatenate([jnp.stack([x, core] + places).astype(jnp.int32), start[::tok]])
    start_rows = jnp.repeat(start.reshape(n, 1, tok), GROUP, axis=2)

    own_swap = lax.ppermute(own, "ctx", swap)
    behind, far, start_rows, info, got[2] = lax.optimization_barrier((behind, far, start_rows, info, got[2]))
    behind_swap, far_swap = [lax.ppermute(v, "ctx", swap) for v in (behind, far)]

    slots = [packed[0]] + [got[e] for e in range(1, n)]
    around_here = (own, behind, far, own_swap, behind_swap, far_swap)
    near, across, *sums = attention(info, start_rows, 0, [slots[0], slots[2]], around_here)
    sent = {2: crossing(across, 2, n, True)}
    right, left, mine, straight, cross = attention(info, start_rows, 1, [slots[1], slots[3]], around_here, sums)
    cross = lax.optimization_barrier((cross, sent))[0]
    crossed = lax.ppermute(cross, "ctx", swap)
    sent[1] = crossing(right, 1, n, True)
    sent[3] = crossing(left, 3, n, True)
    back = along((straight + crossed[1].astype(F32)).astype(BF), -2, everyone)
    back_far = along((cross[2].astype(F32) + crossed[2].astype(F32)).astype(BF), -3, even)
    mine, sent = lax.optimization_barrier((mine + crossed[0].astype(F32), sent))
    total = mine + back.astype(F32) + back_far.astype(F32)
    total = total.astype(BF).reshape(2, n, tok, HD)
    pieces = {
        e: around(lax.dynamic_index_in_dim(total, lax.rem(x + e, n), 1, keepdims=False), e, n)
        for e in (0,) + order
    }
    parts = [near] + [sent[e] for e in range(1, n)]
    xi = lax.optimization_barrier((xi, total))[0]
    ring = [pieces[e] for e in range(n - 1, -1, -1)]
    ring = jnp.stack(ring + ring, axis=0)
    heads = lax.dynamic_slice_in_dim(ring, n - 1 - x, n, 0).transpose(1, 2, 0, 3)
    attended, query_grad = unpack(xi, [v.reshape(2, tok, GROUP, HD) for v in parts])
    return attended, query_grad, heads[0], heads[1]


def solution(mesh):
    spec = P(("ctx", "head"), None, None)
    return jax.shard_map(
        shards,
        mesh=mesh,
        in_specs=(spec, spec, spec, spec, P()),
        out_specs=(spec, spec, spec, spec),
        check_vma=False,
    )
```
